512 devices in a mesh: blk: 64 (over x, z, core), uly: 8 (over y).
Axes of the slice: x: 4, y: 8, z: 8, core: 2. Of those that a mesh axis runs over, the one named last changes fastest.
Arguments:
- queries: bfloat16 [49152, 3072], P(('blk', 'uly')), may hold values from -23 to 23
- keys: bfloat16 [49152, 3072], P(('blk', 'uly')), may hold values from -4.5 to 4.5
- values: bfloat16 [49152, 3072], P(('blk', 'uly')), may hold values from -4.5 to 4.5
- key_lists: int32 [384, 16], P('blk'), may hold values from 0 to 383, as said below
- key_fill: int32 [384], replicated, may hold values from 48 to 96
Outputs:
- attended: bfloat16 [49152, 3072], P(('blk', 'uly'))
The draws below stay inside these ranges and needn't reach their ends.
Inputs may be any that keep to these rules, and one draw needn't show every extreme that they name: `key_lists`: the rows of one aligned block of 3 query tiles (one query cluster) are equal; within a row the tiles t have distinct t // 6; among the rows of one aligned block of 6 query tiles, tiles with equal t // 6 are equal.
All inputs are finite; a program needn't handle non-finite values.
Results may differ from the reference program's by a relative error of at most 0.0047.
Values may be sent and summed in bfloat16 or wider, within the bound.
A program may use at most 128 MiB of HBM per device.

```python
import math
import jax
import jax.numpy as jnp
from jax import lax

H = 24
HD = 128
TILE = 128
SEL = 16
CT = 3
ROWS = 768
LIVE = 96
TOKENS = 49152
QTILES = 384
KTILES = 384


def tile_lists(key):
    per_owner = ROWS // TILE
    blocks = QTILES // per_owner
    clusters = QTILES // CT
    first_key, second_key = jax.random.split(jax.random.fold_in(key, 101))
    designated = jax.random.randint(first_key, (blocks, blocks), 0, per_owner)
    cluster_keys = jax.random.split(second_key, clusters)
    cluster_owners = jax.vmap(lambda row_key: jax.random.permutation(row_key, blocks))(cluster_keys)[:, :SEL]
    tile_cluster = jnp.arange(QTILES, dtype=jnp.int32) // CT
    owner_order = cluster_owners[tile_cluster]
    requester = jnp.arange(QTILES, dtype=jnp.int32) // per_owner
    picked = owner_order * per_owner + designated[requester[:, None], owner_order]
    return picked.astype(jnp.int32)


def key_field(key):
    first_key = jax.random.fold_in(jax.random.fold_in(key, 202), 0)
    normal_part = jnp.clip(jax.random.normal(first_key, (TOKENS, H * HD), jnp.float32), -4.5, 4.5)
    base = normal_part
    tiles = base.reshape(KTILES, TILE, H * HD)
    tiles = tiles.at[:, 4:8].set(tiles[:, 4:8])
    return tiles.reshape(TOKENS, H * HD)


def draw_keys(key, part):
    return key_field(key).astype(jnp.bfloat16)


def draw_queries(key, part):
    key = jax.random.fold_in(key, 303)
    return jnp.clip(jax.random.normal(key, (TOKENS, H * HD), jnp.float32), -4.5, 4.5).astype(jnp.bfloat16)


def draw_key_lists(key, part):
    return tile_lists(key)


def draw_key_fill(key, part):
    key = jax.random.fold_in(key, 404)
    fill = jax.random.randint(key, (KTILES,), LIVE // 2, LIVE + 1)
    first_tile = jnp.arange(KTILES, dtype=jnp.int32) % (ROWS // TILE) == 0
    return jnp.where(first_tile, LIVE, fill).astype(jnp.int32)


def levels(stream_key, shape, cuts, low, top_value):
    loudness = 1.0
    for dim, shards_of in cuts:
        steps = jax.random.uniform(jax.random.fold_in(jax.random.fold_in(stream_key, 6), dim), (shards_of,), jnp.float32, low / len(cuts), top_value / len(cuts))
        loudness = loudness * jnp.repeat(jnp.exp(steps), shape[dim] // shards_of).reshape((-1,) + (1,) * (len(shape) - 1 - dim))
    return loudness


def scatter_about(own_key, shape, width, bound, pieces=(), kind=jnp.bfloat16):
    factor_of = levels(own_key, shape, pieces, -0.22, 0.18) if pieces else 1.0
    values = jax.random.normal(own_key, shape, jnp.float32) * width * factor_of
    return jnp.minimum(jnp.maximum(values, -bound), bound).astype(kind)


def setup_inputs(seed: int = 0) -> dict:
    streams_of = jax.random.split(jax.random.key(seed), 6)
    queries = draw_queries(jax.random.fold_in(streams_of[5], 71), 0)
    keys = draw_keys(jax.random.fold_in(streams_of[5], 71), 0)
    values = scatter_about(streams_of[2], (TOKENS, H * HD), 1.0, 4.5, ((0, 512),))
    key_lists = draw_key_lists(jax.random.fold_in(streams_of[5], 71), 0)
    key_fill = draw_key_fill(jax.random.fold_in(streams_of[5], 71), 0)
    return {"queries": queries, "keys": keys, "values": values, "key_lists": key_lists, "key_fill": key_fill}


def reference(queries, keys, values, key_lists, key_fill):
    score_scale = 1.0 / math.sqrt(HD)
    key_stack = keys.reshape(KTILES, TILE, H, HD)
    value_stack = values.reshape(KTILES, TILE, H, HD)
    query_stack = queries.reshape(QTILES, TILE, H, HD)
    columns = jnp.arange(TILE, dtype=jnp.int32)

    def one_tile(tile_pair):
        query_tile, tile_list = tile_pair
        picked_keys = key_stack[tile_list].astype(jnp.float32)
        picked_values = value_stack[tile_list].astype(jnp.float32)
        live_mask = columns[None, :] < key_fill[tile_list][:, None]
        scores = jnp.einsum('qhd,sthd->hqst', query_tile.astype(jnp.float32), picked_keys) * score_scale
        scores = jnp.where(live_mask[None, None], scores, -1e+30)
        peak = lax.optimization_barrier(jnp.max(scores, axis=(2, 3), keepdims=True))
        weight_raw = jnp.where(live_mask[None, None], jnp.exp(scores - peak), 0.0)
        row_total = lax.optimization_barrier(jnp.sum(weight_raw, axis=(2, 3)))
        weight = lax.optimization_barrier(weight_raw.astype(jnp.bfloat16)).astype(jnp.float32)
        mixture = jnp.einsum('hqst,sthd->qhd', weight, picked_values)
        result = mixture / jnp.transpose(row_total)[:, :, None]
        return result.astype(jnp.bfloat16).reshape(TILE, H * HD)
    attended = lax.map(one_tile, (query_stack, key_lists))
    return attended.reshape(TOKENS, H * HD)
```

```python
import functools
import math

import jax
import jax.numpy as jnp
from jax import lax
from jax.experimental import pallas as pl
from jax.experimental.pallas import tpu as pltpu
from jax.sharding import PartitionSpec as P

HD = 128
TILE = 128
SEL = 16
LIVE = 96
X, Z, C, Y = 4, 8, 2, 8
HX = 3
HEADS = HX * Y
PART = 96
BLOCK = PART * Y
PER = BLOCK // TILE
CROWS = BLOCK // 2
KEYS = SEL * LIVE
GROUPS = LIVE // 32
HALF = X // 2 * PER * GROUPS
HOPS = ((4, 3), (3, 4))
MESH = pl.DeviceIdType.MESH
C2 = math.log2(math.e) / math.sqrt(HD)


def kernel(
    q_ref, k_ref, v_ref, list_ref, fill_ref, out_ref,
    kpack, vpack, kbuf, vbuf, qbuf, obuf, gath, probs, totals, lsend, lrecv, lists,
    p1_send, p1_recv, q_recv, ring_send, ring_recv, sib_send, sib_recv, l_send, l_recv, l_copy, o_send, o_recv,
):
    blk, y = lax.axis_index("blk"), lax.axis_index("uly")
    x, z, c = blk // (Z * C), (blk // C) % Z, blk % C
    plane = z * C + c
    r, a = y % 4, y // 4

    def blk_at(xx):
        return xx * (Z * C) + plane

    barrier = pltpu.get_barrier_semaphore()
    me = x * Y + y

    def greet(j, _):
        p = (me + j) % (X * Y)
        pl.semaphore_signal(barrier, inc=1, device_id=(blk_at(p // Y), p % Y), device_id_type=MESH)
        return 0

    lax.fori_loop(1, X * Y, greet, 0)
    right = (x * (Z * C) + ((z + 1) % Z) * C + c, y)
    left = (x * (Z * C) + ((z + Z - 1) % Z) * C + c, y)
    other = (x * (Z * C) + z * C + (1 - c), y)
    for d in (right, left, other):
        pl.semaphore_signal(barrier, inc=1, device_id=d, device_id_type=MESH)

    first = pl.multiple_of(jnp.where(r == 1, 32, 0), 32)
    second = pl.multiple_of(jnp.where((r == 1) | (r == 2), 64, 32), 32)
    for src, dst in ((k_ref, kpack), (v_ref, vpack)):
        for h in range(HEADS):
            cols = slice(h * HD, (h + 1) * HD)
            dst[h, 0] = src[pl.ds(first, 32), cols]
            dst[h, 1] = src[pl.ds(second, 32), cols]
            dst[h, 2] = src[64:96, cols]
    lsend[...] = jnp.zeros_like(lsend)
    tile = list_ref[...]
    owner = (tile * 10923) >> 16
    place = ((owner & (Z * C - 1)) * X + (owner >> 4)) * PER + tile - owner * PER
    lsend[0:PER, 0:SEL] = tile
    lsend[8 : 8 + PER, 0:SEL] = place * GROUPS

    pl.semaphore_wait(barrier, X * Y - 1 + 3)

    off = ((plane * X + x) * PER + 3 * a) * GROUPS + jnp.where(r == 0, 0, 1 + 2 * r)
    half = x // 2

    def to_heads(i, act):
        yh, xh = (y + 4 + i // HX) % Y, (x + i) % HX
        act(yh * HX + xh, (blk_at(xh), yh), (xh == x) & (yh == y))

    def rows_copy(t, i, rows, wait):
        pack, buf = ((kpack, kbuf), (vpack, vbuf))[t]

        def act(h, device, own):
            src = pack.at[h, pl.ds(0, rows)]
            dst = buf.at[pl.ds(off, rows)]

            @pl.when(jnp.logical_not(own))
            def _():
                copy = pltpu.make_async_remote_copy(
                    src_ref=src, dst_ref=dst, send_sem=p1_send.at[t, i], recv_sem=p1_recv.at[t, half],
                    device_id=device, device_id_type=MESH,
                )
                copy.wait_send() if wait else copy.start()

            if not wait:

                @pl.when(own)
                def _():
                    pltpu.make_async_copy(src, dst, p1_recv.at[t, half]).start()

        to_heads(i, act)

    def q_copy(i, wait):
        def act(h, device, own):
            src = q_ref.at[:, pl.ds(pl.multiple_of(h * HD, HD), HD)]
            dst = qbuf.at[x, pl.ds(pl.multiple_of(y * PART, 32), PART)]

            @pl.when(jnp.logical_not(own))
            def _():
                copy = pltpu.make_async_remote_copy(
                    src_ref=src, dst_ref=dst, send_sem=p1_send.at[2, i], recv_sem=q_recv.at[0],
                    device_id=device, device_id_type=MESH,
                )
                copy.wait_send() if wait else copy.start()

            if not wait:

                @pl.when(own)
                def _():
                    pltpu.make_async_copy(src, dst, q_recv.at[0]).start()

        to_heads(i, act)

    def each_owner(body):
        def step(i, _):
            body(i)
            return 0

        lax.fori_loop(0, HEADS, step, 0)

    def all_rows(t, wait):
        @pl.when(r == 0)
        def _():
            each_owner(lambda i: rows_copy(t, i, 3, wait))

        @pl.when(r != 0)
        def _():
            each_owner(lambda i: rows_copy(t, i, 2, wait))

    all_rows(0, False)
    all_rows(1, False)
    each_owner(lambda i: q_copy(i, False))

    def list_copy(j):
        return pltpu.make_async_remote_copy(
            src_ref=lsend, dst_ref=lrecv.at[x], send_sem=l_send.at[j - 1], recv_sem=l_recv.at[j - 1],
            device_id=(blk_at((x + j) % X), y), device_id_type=MESH,
        )

    def list_arrival(j):
        return pltpu.make_async_remote_copy(
            src_ref=lsend, dst_ref=lrecv.at[(x + X - j) % X], send_sem=l_send.at[j - 1], recv_sem=l_recv.at[j - 1],
            device_id=(blk_at((x + j) % X), y), device_id_type=MESH,
        )

    for j in range(1, X):
        list_copy(j).start()

    def o_copy(n, xq, u, wait):
        src = obuf.at[xq, pl.ds(pl.multiple_of(u * PART, 32), PART)]
        dst = out_ref.at[:, pl.ds(pl.multiple_of((y * HX + x) * HD, HD), HD)]
        own = (xq == x) & (u == y)

        @pl.when(jnp.logical_not(own))
        def _():
            copy = pltpu.make_async_remote_copy(
                src_ref=src, dst_ref=dst, send_sem=o_send.at[n], recv_sem=o_recv.at[0],
                device_id=(blk_at(xq), u), device_id_type=MESH,
            )
            copy.wait_send() if wait else copy.start()

        if not wait:

            @pl.when(own)
            def _():
                pltpu.make_async_copy(src, dst, o_recv.at[0]).start()

    @pl.when(x < HX)
    def _():
        bufs = (kbuf, vbuf)

        def piece(t, zz, core, h):
            return bufs[t].at[pl.ds(((zz * C + core) * 2 + h) * HALF, HALF)]

        def ring(t, way, h, k):
            origin = (z + (Z - (k - 1) if way == 0 else k - 1)) % Z
            part = piece(t, origin, c, h)
            return pltpu.make_async_remote_copy(
                src_ref=part, dst_ref=part, send_sem=ring_send.at[t, way, h, k - 1], recv_sem=ring_recv.at[t, way, h, k - 1],
                device_id=(right, left)[way], device_id_type=MESH,
            )

        def ring_arrival(t, way, h, k):
            origin = (z + (Z - k if way == 0 else k)) % Z
            part = piece(t, origin, c, h)
            return pltpu.make_async_remote_copy(
                src_ref=part, dst_ref=part, send_sem=ring_send.at[t, way, h, k - 1], recv_sem=ring_recv.at[t, way, h, k - 1],
                device_id=(right, left)[way], device_id_type=MESH,
            )

        def sibling(t, shift, h, core):
            part = piece(t, (z + shift) % Z, core, h)
            return pltpu.make_async_remote_copy(
                src_ref=part, dst_ref=part, send_sem=sib_send.at[t, shift, h], recv_sem=sib_recv.at[t, shift, h],
                device_id=other, device_id_type=MESH,
            )

        def own_part(t, h):
            part = piece(t, z, c, h)
            pltpu.make_async_copy(part, part, p1_recv.at[t, h]).wait()
            for way in (0, 1):
                ring(t, way, h, 1).start()
            sibling(t, 0, h, c).start()

        def pass_on(t, h, k):
            for way in (0, 1):
                if k > HOPS[h][way]:
                    continue
                ring_arrival(t, way, h, k).wait_recv()
                if k < HOPS[h][way]:
                    ring(t, way, h, k + 1).start()
                sibling(t, (Z - k) if way == 0 else k, h, c).start()

        def gather(i, buf):
            xq, s = (x + i // 2) % X, i % 2
            for j in range(SEL):
                at = lists[xq, 8 + 3 * s, j]
                gath[j * LIVE : (j + 1) * LIVE, :] = buf[pl.ds(at, GROUPS)].reshape(LIVE, HD)
            return xq, s

        def scores(i, _):
            xq, s = gather(i, kbuf)
            lane = lax.broadcasted_iota(jnp.int32, (1, KEYS), 1)
            end = jnp.zeros((1, KEYS), jnp.int32)
            for j in range(SEL):
                end = jnp.where(lane >= j * LIVE, fill_ref[lists[xq, 3 * s, j]] + j * LIVE, end)
            bias = jnp.where(lane < end, 0.0, -1e30)
            for n in range(3):
                rows = pl.ds(pl.multiple_of(s * CROWS + n * TILE, TILE), TILE)
                sc = lax.dot_general(
                    qbuf[xq, rows, :], gath[...], (((1,), (1,)), ((), ())), preferred_element_type=jnp.float32
                )
                sc = sc + bias
                peak = jnp.max(sc, axis=1, keepdims=True)
                w = jnp.exp2((sc - peak) * C2)
                totals[i, n * TILE : (n + 1) * TILE, :] = jnp.sum(w, axis=1, keepdims=True)
                probs[i, n * TILE : (n + 1) * TILE, :] = w.astype(jnp.bfloat16)
            return 0

        def mix(i, _):
            xq, s = gather(i, vbuf)
            for n in range(3):
                rows = pl.ds(pl.multiple_of(s * CROWS + n * TILE, TILE), TILE)
                o = jnp.dot(probs[i, n * TILE : (n + 1) * TILE, :], gath[...], preferred_element_type=jnp.float32)
                obuf[xq, rows, :] = (o / totals[i, n * TILE : (n + 1) * TILE, :]).astype(jnp.bfloat16)
            for w in range(4):
                o_copy(4 * i + w, xq, 4 * s + w, False)
            return 0

        for h in (0, 1):
            own_part(0, h)
        for k in range(1, 4):
            for h in (0, 1):
                pass_on(0, h, k)
        for h in (0, 1):
            own_part(1, h)
        for h in (0, 1):
            pass_on(0, h, 4)
        for j in range(1, X):
            list_arrival(j).wait_recv()
        lrecv[pl.ds(x, 1)] = lsend[...][None]
        copy = pltpu.make_async_copy(lrecv, lists, l_copy.at[0])
        copy.start()
        copy.wait()
        pltpu.make_async_copy(qbuf, qbuf, q_recv.at[0]).wait()
        for shift in range(Z):
            for h in (0, 1):
                sibling(0, shift, h, 1 - c).wait_recv()
        lax.fori_loop(0, 4, scores, 0)
        pass_on(1, 0, 1)
        lax.fori_loop(4, 6, scores, 0)
        pass_on(1, 1, 1)
        lax.fori_loop(6, 8, scores, 0)
        for k in range(2, 5):
            for h in (0, 1):
                pass_on(1, h, k)
        for shift in range(Z):
            for h in (0, 1):
                sibling(1, shift, h, 1 - c).wait_recv()
        lax.fori_loop(0, 8, mix, 0)

        for t in (0, 1):
            for h in (0, 1):
                for way in (0, 1):
                    for k in range(1, HOPS[h][way] + 1):
                        ring(t, way, h, k).wait_send()
                for shift in range(Z):
                    sibling(t, shift, h, c).wait_send()

        def sent(i, _):
            for w in range(4):
                o_copy(4 * i + w, (x + i // 2) % X, 4 * (i % 2) + w, True)
            return 0

        lax.fori_loop(0, 8, sent, 0)

    @pl.when(x == HX)
    def _():
        for j in range(1, X):
            list_arrival(j).wait_recv()

    all_rows(0, True)
    all_rows(1, True)
    each_owner(lambda i: q_copy(i, True))
    for j in range(1, X):
        list_copy(j).wait_send()
    pltpu.make_async_copy(out_ref, out_ref, o_recv.at[0]).wait()


def local(queries, keys, values, key_lists, key_fill):
    bf = jnp.bfloat16
    vmem = pl.BlockSpec(memory_space=pltpu.VMEM)
    return pl.pallas_call(
        kernel,
        out_shape=jax.ShapeDtypeStruct(queries.shape, bf),
        in_specs=[vmem, vmem, vmem, vmem, pl.BlockSpec(memory_space=pltpu.SMEM)],
        out_specs=pl.BlockSpec(memory_space=pl.ANY),
        scratch_shapes=[
            pltpu.VMEM((HEADS, GROUPS, 32, HD), bf),
            pltpu.VMEM((HEADS, GROUPS, 32, HD), bf),
            pltpu.VMEM((Z * C * X * PER * GROUPS, 32, HD), bf),
            pltpu.VMEM((Z * C * X * PER * GROUPS, 32, HD), bf),
            pltpu.VMEM((X, BLOCK, HD), bf),
            pltpu.VMEM((X, BLOCK, HD), bf),
            pltpu.VMEM((KEYS, HD), bf),
            pltpu.VMEM((2 * X, CROWS, KEYS), bf),
            pltpu.VMEM((2 * X, CROWS, 1), jnp.float32),
            pltpu.VMEM((16, 128), jnp.int32),
            pltpu.VMEM((X, 16, 128), jnp.int32),
            pltpu.SMEM((X, 16, 128), jnp.int32),
            pltpu.SemaphoreType.DMA((3, HEADS)),
            pltpu.SemaphoreType.DMA((2, 2)),
            pltpu.SemaphoreType.DMA((1,)),
            pltpu.SemaphoreType.DMA((2, 2, 2, 4)),
            pltpu.SemaphoreType.DMA((2, 2, 2, 4)),
            pltpu.SemaphoreType.DMA((2, Z, 2)),
            pltpu.SemaphoreType.DMA((2, Z, 2)),
            pltpu.SemaphoreType.DMA((X - 1,)),
            pltpu.SemaphoreType.DMA((X - 1,)),
            pltpu.SemaphoreType.DMA((1,)),
            pltpu.SemaphoreType.DMA((X * Y,)),
            pltpu.SemaphoreType.DMA((1,)),
        ],
        compiler_params=pltpu.CompilerParams(
            collective_id=0, has_side_effects=True, vmem_limit_bytes=56 * 1024 * 1024
        ),
        cost_estimate=pl.CostEstimate(flops=5_000_000_000, bytes_accessed=4_000_000, transcendentals=4_800_000),
    )(queries, keys, values, key_lists, key_fill)


def solution(mesh):
    in_specs = (
        P(("blk", "uly"), None),
        P(("blk", "uly"), None),
        P(("blk", "uly"), None),
        P("blk", None),
        P(),
    )
    out_specs = P(("blk", "uly"), None)
    return jax.shard_map(local, mesh=mesh, in_specs=in_specs, out_specs=out_specs, check_vma=False)
```

```python
import math

import jax
import jax.numpy as jnp
from jax import lax
from jax.experimental import pallas as pl
from jax.experimental.pallas import tpu as pltpu
from jax.sharding import PartitionSpec as P

HD = 128
TILE = 128
SEL = 16
LIVE = 96
X, Z, C, Y = 4, 8, 2, 8
HX = 3
HEADS = HX * Y
PART = 96
BLOCK = PART * Y
PER = BLOCK // TILE
CROWS = BLOCK // 2
KEYS = SEL * LIVE
GROUPS = LIVE // 32
SLOTS = 26
CHUNK = SLOTS * GROUPS
HALF = 10 * GROUPS
HALF3 = 6 * GROUPS
GUEST = 18 * GROUPS
LATE = 20 * GROUPS
HOPS = ((4, 3), (3, 4))
MESH = pl.DeviceIdType.MESH
C2 = math.log2(math.e) / math.sqrt(HD)


def kernel(
    q_ref, k_ref, v_ref, list_ref, fill_ref, out_ref,
    qin, kin, vin, kpack, vpack, kbuf, vbuf, qbuf, obuf, rbuf, gath, probs, totals, lsend, lrecv, lists,
    in_sem, p1_send, p1_recv, q_recv, ring_send, ring_recv, sib_send, sib_recv, dl_send, dl_recv, ds_send, ds_recv,
    l_send, l_recv, l_copy, o_send, o_recv, r_send, r_recv,
):
    blk, y = lax.axis_index("blk"), lax.axis_index("uly")
    x, z, c = blk // (Z * C), (blk // C) % Z, blk % C
    plane = z * C + c
    r, a = y % 4, y // 4

    reads = [
        pltpu.make_async_copy(src, dst, in_sem.at[n])
        for n, (src, dst) in enumerate(((k_ref, kin), (v_ref, vin), (q_ref, qin)))
    ]
    for copy in reads:
        copy.start()

    def blk_at(xx):
        return xx * (Z * C) + plane

    barrier = pltpu.get_barrier_semaphore()
    me = x * Y + y

    def greet(j, _):
        p = (me + j) % (X * Y)
        pl.semaphore_signal(barrier, inc=1, device_id=(blk_at(p // Y), p % Y), device_id_type=MESH)
        return 0

    lax.fori_loop(1, X * Y, greet, 0)
    right = (x * (Z * C) + ((z + 1) % Z) * C + c, y)
    left = (x * (Z * C) + ((z + Z - 1) % Z) * C + c, y)
    other = (x * (Z * C) + z * C + (1 - c), y)
    for d in (right, left, other):
        pl.semaphore_signal(barrier, inc=1, device_id=d, device_id_type=MESH)

    lsend[...] = jnp.zeros_like(lsend)
    tile = list_ref[...]
    owner = (tile * 10923) >> 16
    n = tile - owner * PER
    ox = owner >> 4
    start = (owner & (Z * C - 1)) * SLOTS
    edge = ox * PER + n + jnp.where(ox == 3, 2, 0)
    first = (n == 0) | (n == 3)
    outer = jnp.where(first, 20 + ox + jnp.where(n == 3, 1, 0), ox * 5 + n - 1 - jnp.where(n > 3, 1, 0))
    inner = jnp.where(ox == 1, 4, 14) + n
    middle = jnp.where((ox == 0) | (ox == 2), outer, inner)
    lsend[0:PER, 0:SEL] = tile
    lsend[8 : 8 + PER, 0:SEL] = (start + edge) * GROUPS
    lsend[16 : 16 + PER, 0:SEL] = (start + middle) * GROUPS

    piece0 = pl.multiple_of(jnp.where(r == 1, 32, 0), 32)
    piece1 = pl.multiple_of(jnp.where((r == 1) | (r == 2), 64, 32), 32)

    def pack(t):
        src, dst = ((kin, kpack), (vin, vpack))[t]
        reads[t].wait()
        for h in range(HEADS):
            cols = slice(h * HD, (h + 1) * HD)
            dst[h, 0] = src[pl.ds(piece0, 32), cols]
            dst[h, 1] = src[pl.ds(piece1, 32), cols]
            dst[h, 2] = src[64:96, cols]

    pack(0)
    pl.semaphore_wait(barrier, X * Y - 1 + 3)

    bufs = (kbuf, vbuf)

    def region(t, zz, core, at, count):
        return bufs[t].at[pl.ds((zz * C + core) * CHUNK + at, count)]

    off = jnp.where(r == 0, 0, 1 + 2 * r)
    wing = (x == 0) | (x == 2)
    i32 = jnp.int32

    def target(xh):
        if xh != 1:
            helped = x == 3
            xd = jnp.where(helped, 3, xh)
            at = jnp.where(helped, (PER if xh else 0), x * PER) * GROUPS + 9 * a + off
            half = jnp.where(helped, xh // 2, jnp.where((x == 2) | ((x == 1) & (a == 1) & (r != 0)), 1, 0))
            return xd, at, half
        guest = wing & (r == 0)
        xd = jnp.where(guest, x, 1)
        own = jnp.where(wing, 5 * x * GROUPS + 6 * a + off - 3, jnp.where(x == 1, 4, 14) * GROUPS + 9 * a + off)
        at = jnp.where(guest, GUEST + GROUPS * a, own)
        half = jnp.where(guest, 1, jnp.where(x >= 2, 1, 0))
        return xd, at, half

    targets = [target(xh) for xh in range(HX)]

    def rows_copy(t, i, rows, wait):
        yh = (y + 4 + i) % Y
        for xh, (xd, at, half) in enumerate(targets):
            own = (xd == x) & (yh == y)
            src = (kpack, vpack)[t].at[yh * HX + xh, pl.ds(0, rows)]
            dst = region(t, z, c, at, rows)

            @pl.when(jnp.logical_not(own))
            def _():
                copy = pltpu.make_async_remote_copy(
                    src_ref=src, dst_ref=dst, send_sem=p1_send.at[t, i * HX + xh], recv_sem=p1_recv.at[t, half],
                    device_id=(blk_at(xd), yh), device_id_type=MESH,
                )
                copy.wait_send() if wait else copy.start()

            if not wait:

                @pl.when(own)
                def _():
                    pltpu.make_async_copy(src, dst, p1_recv.at[t, half]).start()

    def q_copy(i, wait):
        yh = (y + 4 + i) % Y
        for xh in range(HX):
            own = (xh == x) & (yh == y)
            src = qin.at[:, pl.ds(pl.multiple_of((yh * HX + xh) * HD, HD), HD)]
            dst = qbuf.at[x, pl.ds(pl.multiple_of(y * PART, 32), PART)]

            @pl.when(jnp.logical_not(own))
            def _():
                copy = pltpu.make_async_remote_copy(
                    src_ref=src, dst_ref=dst, send_sem=p1_send.at[2, i * HX + xh], recv_sem=q_recv.at[0],
                    device_id=(blk_at(xh), yh), device_id_type=MESH,
                )
                copy.wait_send() if wait else copy.start()

            if not wait:

                @pl.when(own)
                def _():
                    pltpu.make_async_copy(src, dst, q_recv.at[0]).start()

    def each_y(body):
        def step(i, _):
            body(i)
            return 0

        lax.fori_loop(0, Y, step, 0)

    def all_rows(t, wait):
        @pl.when(r == 0)
        def _():
            each_y(lambda i: rows_copy(t, i, 3, wait))

        @pl.when(r != 0)
        def _():
            each_y(lambda i: rows_copy(t, i, 2, wait))

    all_rows(0, False)

    def list_copy(j):
        return pltpu.make_async_remote_copy(
            src_ref=lsend, dst_ref=lrecv.at[x], send_sem=l_send.at[j - 1], recv_sem=l_recv.at[j - 1],
            device_id=(blk_at((x + j) % X), y), device_id_type=MESH,
        )

    def list_arrival(j):
        return pltpu.make_async_remote_copy(
            src_ref=lsend, dst_ref=lrecv.at[(x + X - j) % X], send_sem=l_send.at[j - 1], recv_sem=l_recv.at[j - 1],
            device_id=(blk_at((x + j) % X), y), device_id_type=MESH,
        )

    for j in range(1, X):
        list_copy(j).start()

    def ring_copy(t, way, h, k, size, distance):
        origin = (z + (Z - distance if way == 0 else distance)) % Z
        part = region(t, origin, c, size * h, size)
        return pltpu.make_async_remote_copy(
            src_ref=part, dst_ref=part, send_sem=ring_send.at[t, way, h, k - 1], recv_sem=ring_recv.at[t, way, h, k - 1],
            device_id=(right, left)[way], device_id_type=MESH,
        )

    def sibling(t, shift, h, core):
        part = region(t, (z + shift) % Z, core, HALF * h, HALF)
        return pltpu.make_async_remote_copy(
            src_ref=part, dst_ref=part, send_sem=sib_send.at[t, shift, h], recv_sem=sib_recv.at[t, shift, h],
            device_id=other, device_id_type=MESH,
        )

    def guest(t, shift):
        origin = (z + shift) % Z
        return pltpu.make_async_remote_copy(
            src_ref=region(t, origin, c, GUEST, 2 * GROUPS), dst_ref=region(t, origin, c, LATE + GROUPS * x, 2 * GROUPS),
            send_sem=dl_send.at[t, shift, 0], recv_sem=dl_recv.at[t, shift, x // 2],
            device_id=(blk_at(1), y), device_id_type=MESH,
        )

    def hand_over(t, shift, h):
        origin = (z + shift) % Z
        return pltpu.make_async_remote_copy(
            src_ref=region(t, origin, c, HALF3 * h, HALF3), dst_ref=region(t, origin, c, LATE, HALF3),
            send_sem=dl_send.at[t, shift, h], recv_sem=dl_recv.at[t, shift, 0],
            device_id=(blk_at(2 * h), y), device_id_type=MESH,
        )

    def late_sibling(t, shift, core, tiles):
        part = region(t, (z + shift) % Z, core, LATE, tiles * GROUPS)
        return pltpu.make_async_remote_copy(
            src_ref=part, dst_ref=part, send_sem=ds_send.at[t, shift], recv_sem=ds_recv.at[t, shift],
            device_id=other, device_id_type=MESH,
        )

    def spread(t, shift, h):
        sibling(t, shift, h, c).start()
        if h == 1:

            @pl.when(x != 1)
            def _():
                guest(t, shift).start()

    def late(t, shift):
        @pl.when(x != 1)
        def _():
            part = region(t, (z + shift) % Z, c, LATE, HALF3)
            pltpu.make_async_copy(part, part, dl_recv.at[t, shift, 0]).wait()
            late_sibling(t, shift, c, 6).start()

        @pl.when(x == 1)
        def _():
            for n in (0, 1):
                part = region(t, (z + shift) % Z, c, LATE + 2 * GROUPS * n, 2 * GROUPS)
                pltpu.make_async_copy(part, part, dl_recv.at[t, shift, n]).wait()
            late_sibling(t, shift, c, 4).start()

    def own_part(t, h, helper):
        size = HALF3 if helper else HALF
        part = region(t, z, c, size * h, size)
        pltpu.make_async_copy(part, part, p1_recv.at[t, h]).wait()
        for way in (0, 1):
            ring_copy(t, way, h, 1, size, 0).start()
        hand_over(t, 0, h).start() if helper else spread(t, 0, h)

    def pass_on(t, h, k, helper):
        size = HALF3 if helper else HALF
        for way in (0, 1):
            if k > HOPS[h][way]:
                continue
            ring_copy(t, way, h, k, size, k).wait_recv()
            if k < HOPS[h][way]:
                ring_copy(t, way, h, k + 1, size, k).start()
            shift = (Z - k) if way == 0 else k
            hand_over(t, shift, h).start() if helper else spread(t, shift, h)

    def ring_sent(t, helper):
        size = HALF3 if helper else HALF
        for h in (0, 1):
            for way in (0, 1):
                for k in range(1, HOPS[h][way] + 1):
                    ring_copy(t, way, h, k, size, k - 1).wait_send()

    @pl.when(x < HX)
    def _():
        for h in (0, 1):
            own_part(0, h, False)

    @pl.when(x == HX)
    def _():
        for h in (0, 1):
            own_part(0, h, True)

    pack(1)
    all_rows(1, False)
    reads[2].wait()
    each_y(lambda i: q_copy(i, False))

    def o_copy(n, src, xq, u, xh, wait):
        dst = out_ref.at[:, pl.ds(pl.multiple_of((y * HX + xh) * HD, HD), HD)]
        own = (xq == x) & (u == y)

        @pl.when(jnp.logical_not(own))
        def _():
            copy = pltpu.make_async_remote_copy(
                src_ref=src, dst_ref=dst, send_sem=o_send.at[n], recv_sem=o_recv.at[0],
                device_id=(blk_at(xq), u), device_id_type=MESH,
            )
            copy.wait_send() if wait else copy.start()

        if not wait:

            @pl.when(own)
            def _():
                pltpu.make_async_copy(src, dst, o_recv.at[0]).start()

    @pl.when(x < HX)
    def _():
        place = jnp.where(x == 1, 16, 8)

        def cluster(i):
            return jnp.where(i < 2, 3, (x + i // 2) % HX), i % 2

        def gather(i, buf):
            xq, s = cluster(i)
            for j in range(SEL):
                at = lists[xq, place + 3 * s, j]
                gath[j * LIVE : (j + 1) * LIVE, :] = buf[pl.ds(at, GROUPS)].reshape(LIVE, HD)
            return xq, s

        def scores(i, _):
            xq, s = gather(i, kbuf)
            lane = lax.broadcasted_iota(jnp.int32, (1, KEYS), 1)
            end = jnp.zeros((1, KEYS), jnp.int32)
            for j in range(SEL):
                end = jnp.where(lane >= j * LIVE, fill_ref[lists[xq, 3 * s, j]] + j * LIVE, end)
            bias = jnp.where(lane < end, 0.0, -1e30)
            for n in range(3):
                rows = pl.ds(pl.multiple_of(s * CROWS + n * TILE, TILE), TILE)
                sc = lax.dot_general(
                    qbuf[xq, rows, :], gath[...], (((1,), (1,)), ((), ())), preferred_element_type=jnp.float32
                )
                sc = sc + bias
                peak = jnp.max(sc, axis=1, keepdims=True)
                w = jnp.exp2((sc - peak) * C2)
                totals[i, n * TILE : (n + 1) * TILE, :] = jnp.sum(w, axis=1, keepdims=True)
                probs[i, n * TILE : (n + 1) * TILE, :] = w.astype(jnp.bfloat16)
            return 0

        def block_piece(xq, u):
            return obuf.at[xq, pl.ds(pl.multiple_of(u * PART, 32), PART)]

        def relay(s):
            part = pl.ds(s * CROWS, CROWS)
            return pltpu.make_async_remote_copy(
                src_ref=obuf.at[HX, part], dst_ref=rbuf.at[x, part], send_sem=r_send.at[s], recv_sem=r_recv.at[x, s],
                device_id=(blk_at(HX), y), device_id_type=MESH,
            )

        def mix(i, _):
            xq, s = gather(i, vbuf)
            for n in range(3):
                rows = pl.ds(pl.multiple_of(s * CROWS + n * TILE, TILE), TILE)
                o = jnp.dot(probs[i, n * TILE : (n + 1) * TILE, :], gath[...], preferred_element_type=jnp.float32)
                obuf[xq, rows, :] = (o / totals[i, n * TILE : (n + 1) * TILE, :]).astype(jnp.bfloat16)
            return xq, s

        def mix_and_send(i, _):
            xq, s = mix(i, 0)
            for w in range(4):
                o_copy(4 * i + w, block_piece(xq, 4 * s + w), xq, 4 * s + w, x, False)
            return 0

        for k in range(1, 4):
            for h in (0, 1):
                pass_on(0, h, k, False)
            for shift in {k - 1, (Z - k + 1) % Z}:
                late(0, shift)
        for h in (0, 1):
            own_part(1, h, False)
        for h in (0, 1):
            pass_on(0, h, 4, False)
        for shift in (3, 5, 4):
            late(0, shift)
        for j in range(1, X):
            list_arrival(j).wait_recv()
        lrecv[pl.ds(x, 1)] = lsend[...][None]
        copy = pltpu.make_async_copy(lrecv, lists, l_copy.at[0])
        copy.start()
        copy.wait()
        pltpu.make_async_copy(qbuf, qbuf, q_recv.at[0]).wait()

        def from_sibling(t):
            for shift in range(Z):
                for h in (0, 1):
                    sibling(t, shift, h, 1 - c).wait_recv()

                @pl.when(x != 1)
                def _():
                    late_sibling(t, shift, 1 - c, 6).wait_recv()

                @pl.when(x == 1)
                def _():
                    late_sibling(t, shift, 1 - c, 4).wait_recv()

        from_sibling(0)
        lax.fori_loop(0, 4, scores, 0)
        pass_on(1, 0, 1, False)
        lax.fori_loop(4, 6, scores, 0)
        pass_on(1, 1, 1, False)
        lax.fori_loop(6, 8, scores, 0)
        late(1, 0)
        for k in range(2, 5):
            for h in (0, 1):
                pass_on(1, h, k, False)
            for shift in {k - 1, Z - k + 1}:
                late(1, shift)
        late(1, 4)
        from_sibling(1)
        for s in (0, 1):
            mix(s, 0)
            relay(s).start()
        lax.fori_loop(2, 8, mix_and_send, 0)

        for t in (0, 1):
            ring_sent(t, False)
            for shift in range(Z):
                for h in (0, 1):
                    sibling(t, shift, h, c).wait_send()

                @pl.when(x != 1)
                def _():
                    guest(t, shift).wait_send()
                    late_sibling(t, shift, c, 6).wait_send()

                @pl.when(x == 1)
                def _():
                    late_sibling(t, shift, c, 4).wait_send()

        for s in (0, 1):
            relay(s).wait_send()

        def sent(i, _):
            xq, s = cluster(i)
            for w in range(4):
                o_copy(4 * i + w, block_piece(xq, 4 * s + w), xq, 4 * s + w, x, True)
            return 0

        lax.fori_loop(2, 8, sent, 0)

    @pl.when(x == HX)
    def _():
        for k in range(1, 4):
            for h in (0, 1):
                pass_on(0, h, k, True)
        for h in (0, 1):
            own_part(1, h, True)
        for h in (0, 1):
            pass_on(0, h, 4, True)
        for k in range(1, 5):
            for h in (0, 1):
                pass_on(1, h, k, True)
        for j in range(1, X):
            list_arrival(j).wait_recv()
        for t in (0, 1):
            ring_sent(t, True)
            for shift in range(Z):
                for h in (0, 1):
                    hand_over(t, shift, h).wait_send()

        def column(wait):
            for s in (0, 1):
                for xh in range(HX):
                    if not wait:
                        part = rbuf.at[xh, pl.ds(s * CROWS, CROWS)]
                        pltpu.make_async_copy(part, part, r_recv.at[xh, s]).wait()
                    for w in range(4):
                        u = 4 * s + w
                        o_copy((s * HX + xh) * 4 + w, rbuf.at[xh, pl.ds(u * PART, PART)], x, u, xh, wait)

        column(False)
        column(True)

    all_rows(0, True)
    all_rows(1, True)
    each_y(lambda i: q_copy(i, True))
    for j in range(1, X):
        list_copy(j).wait_send()
    pltpu.make_async_copy(out_ref, out_ref, o_recv.at[0]).wait()


def local(queries, keys, values, key_lists, key_fill):
    bf = jnp.bfloat16
    anywhere = pl.BlockSpec(memory_space=pl.ANY)
    dma = pltpu.SemaphoreType.DMA
    return pl.pallas_call(
        kernel,
        out_shape=jax.ShapeDtypeStruct(queries.shape, bf),
        in_specs=[
            anywhere, anywhere, anywhere,
            pl.BlockSpec(memory_space=pltpu.VMEM), pl.BlockSpec(memory_space=pltpu.SMEM),
        ],
        out_specs=anywhere,
        scratch_shapes=[
            pltpu.VMEM((PART, HEADS * HD), bf),
            pltpu.VMEM((PART, HEADS * HD), bf),
            pltpu.VMEM((PART, HEADS * HD), bf),
            pltpu.VMEM((HEADS, GROUPS, 32, HD), bf),
            pltpu.VMEM((HEADS, GROUPS, 32, HD), bf),
            pltpu.VMEM((Z * C * CHUNK, 32, HD), bf),
            pltpu.VMEM((Z * C * CHUNK, 32, HD), bf),
            pltpu.VMEM((X, BLOCK, HD), bf),
            pltpu.VMEM((X, BLOCK, HD), bf),
            pltpu.VMEM((HX, BLOCK, HD), bf),
            pltpu.VMEM((KEYS, HD), bf),
            pltpu.VMEM((2 * X, CROWS, KEYS), bf),
            pltpu.VMEM((2 * X, CROWS, 1), jnp.float32),
            pltpu.VMEM((24, 128), jnp.int32),
            pltpu.VMEM((X, 24, 128), jnp.int32),
            pltpu.SMEM((X, 24, 128), jnp.int32),
            dma((3,)),
            dma((3, HEADS)),
            dma((2, 2)),
            dma((1,)),
            dma((2, 2, 2, 4)),
            dma((2, 2, 2, 4)),
            dma((2, Z, 2)),
            dma((2, Z, 2)),
            dma((2, Z, 2)),
            dma((2, Z, 2)),
            dma((2, Z)),
            dma((2, Z)),
            dma((X - 1,)),
            dma((X - 1,)),
            dma((1,)),
            dma((X * Y,)),
            dma((1,)),
            dma((2,)),
            dma((HX, 2)),
        ],
        compiler_params=pltpu.CompilerParams(
            collective_id=0, has_side_effects=True, vmem_limit_bytes=56 * 1024 * 1024
        ),
        cost_estimate=pl.CostEstimate(flops=5_000_000_000, bytes_accessed=4_000_000, transcendentals=4_800_000),
    )(queries, keys, values, key_lists, key_fill)


def solution(mesh):
    in_specs = (
        P(("blk", "uly"), None),
        P(("blk", "uly"), None),
        P(("blk", "uly"), None),
        P("blk", None),
        P(),
    )
    out_specs = P(("blk", "uly"), None)
    return jax.shard_map(local, mesh=mesh, in_specs=in_specs, out_specs=out_specs, check_vma=False)
```

```python
import math

import jax
import jax.numpy as jnp
from jax import lax
from jax.experimental import pallas as pl
from jax.experimental.pallas import tpu as pltpu
from jax.sharding import PartitionSpec as P

HD = 128
TILE = 128
SEL = 16
LIVE = 96
X, Z, C, Y = 4, 8, 2, 8
HX = 3
HEADS = HX * Y
PART = 96
BLOCK = PART * Y
PER = BLOCK // TILE
CROWS = BLOCK // 2
KEYS = SEL * LIVE
GROUPS = LIVE // 32
EDGE, MID, HELP = 0, 1, 2
BASE = (0, 34)
SIZE = {EDGE: (34, 26), MID: (32, 28), HELP: (20, 16)}
OWN = {EDGE: (30, 24), MID: (32, 28)}
LATE = 62
LATES = {EDGE: (10, 8), MID: (8, 4)}
CHUNK = 80
HOPS = ((4, 3), (3, 4))
MESH = pl.DeviceIdType.MESH
C2 = math.log2(math.e) / math.sqrt(HD)


def kernel(
    q_ref, k_ref, v_ref, list_ref, fill_ref, out_ref,
    qin, kin, vin, kpack, vpack, kbuf, vbuf, qbuf, obuf, rbuf, gath, probs, totals, lsend, lrecv, lists,
    in_sem, p1_send, p1_recv, q_recv, ring_send, ring_recv, sib_send, sib_recv, dl_send, dl_recv, ds_send, ds_recv,
    l_send, l_recv, l_copy, o_send, o_recv, r_send, r_recv,
):
    blk, y = lax.axis_index("blk"), lax.axis_index("uly")
    x, z, c = blk >> 4, (blk >> 1) & 7, blk & 1
    plane = blk & 15
    r, a = y & 3, y >> 2
    role_of = ((x & 1) == 0, x == 1, x == 3)

    def by_role(f, roles=(EDGE, MID, HELP)):
        for role in roles:
            pl.when(role_of[role])(lambda role=role: f(role))

    reads = [
        pltpu.make_async_copy(src, dst, in_sem.at[n])
        for n, (src, dst) in enumerate(((k_ref, kin), (v_ref, vin), (q_ref, qin)))
    ]
    for copy in reads:
        copy.start()

    def blk_at(xx):
        return (xx << 4) + plane

    barrier = pltpu.get_barrier_semaphore()
    right = ((blk & 49) + (((z + 1) & 7) << 1), y)
    left = ((blk & 49) + (((z + 7) & 7) << 1), y)
    other = (blk ^ 1, y)
    near = [(blk_at((x + i) & 3), (y + j) & 7) for j in range(Y) for i in range(X) if i or j]
    for d in (right, left, other, *near):
        pl.semaphore_signal(barrier, inc=1, device_id=d, device_id_type=MESH)

    piece0 = pl.multiple_of(jnp.where(r == 1, 32, 0), 32)
    piece1 = pl.multiple_of(jnp.where((r == 1) | (r == 2), 64, 32), 32)

    def pack(t):
        src, dst = ((kin, kpack), (vin, vpack))[t]
        reads[t].wait()
        for h in range(HEADS):
            cols = slice(h * HD, (h + 1) * HD)
            dst[h, 0] = src[pl.ds(piece0, 32), cols]
            dst[h, 1] = src[pl.ds(piece1, 32), cols]
            dst[h, 2] = src[64:96, cols]

    pack(0)
    pl.semaphore_wait(barrier, len(near) + 3)

    bufs = (kbuf, vbuf)

    def region(t, zz, core, at, count):
        return bufs[t].at[pl.ds((zz * C + core) * CHUNK + at, count)]

    off = jnp.where(r == 0, 0, 1 + r)
    wing = (x & 1) == 0

    def pick(values):
        out = values[-1]
        for n in range(len(values) - 1):
            out = jnp.where(x == n, values[n], out)
        return out

    def target(xh):
        if xh != 1:
            side = 1 if xh else 0
            return (
                jnp.where(x == 3, 3, xh),
                pick((0, 10, 20, 10 * side)) + 5 * a + off,
                BASE[1] + pick((0, 8, 16, 8 * side)) + 4 * a + r,
            )
        guest = wing & (r == 0)
        at0 = jnp.where(wing, 3 * a + r - 1, 5 * a + off) + pick((0, 6, 16, 22))
        at1 = jnp.where(wing, 3 * a + r - 1, 4 * a + r) + pick((0, 6, 14, 20))
        return (
            jnp.where(guest, x, 1),
            jnp.where(guest, OWN[EDGE][0] + 2 * a, at0),
            BASE[1] + jnp.where(guest, OWN[EDGE][1] + a, at1),
        )

    targets = [target(xh) for xh in range(HX)]
    second = jnp.where(r == 0, 2, 1)

    def rows_copy(t, h, i, rows, wait):
        yh = (y + 4 + i) & 7
        for xh, (xd, *at) in enumerate(targets):
            own = (xd == x) & (yh == y)
            src = (kpack, vpack)[t].at[yh * HX + xh, pl.ds(second if h else 0, rows)]
            dst = region(t, z, c, at[h], rows)

            @pl.when(jnp.logical_not(own))
            def _():
                copy = pltpu.make_async_remote_copy(
                    src_ref=src, dst_ref=dst, send_sem=p1_send.at[2 * t + h, i * HX + xh], recv_sem=p1_recv.at[t, h],
                    device_id=(blk_at(xd), yh), device_id_type=MESH,
                )
                copy.wait_send() if wait else copy.start()

            if not wait:

                @pl.when(own)
                def _():
                    pltpu.make_async_copy(src, dst, p1_recv.at[t, h]).start()

    def q_copy(i, wait):
        yh = (y + 4 + i) & 7
        for xh in range(HX):
            own = (xh == x) & (yh == y)
            src = qin.at[:, pl.ds(pl.multiple_of((yh * HX + xh) * HD, HD), HD)]
            dst = qbuf.at[x, pl.ds(pl.multiple_of(y * PART, 32), PART)]

            @pl.when(jnp.logical_not(own))
            def _():
                copy = pltpu.make_async_remote_copy(
                    src_ref=src, dst_ref=dst, send_sem=p1_send.at[4, i * HX + xh], recv_sem=q_recv.at[0],
                    device_id=(blk_at(xh), yh), device_id_type=MESH,
                )
                copy.wait_send() if wait else copy.start()

            if not wait:

                @pl.when(own)
                def _():
                    pltpu.make_async_copy(src, dst, q_recv.at[0]).start()

    def each_y(body):
        def step(i, _):
            body(i)
            return 0

        lax.fori_loop(0, Y, step, 0)

    def all_rows(t, h, wait):
        if h == 1:
            each_y(lambda i: rows_copy(t, h, i, 1, wait))
            return

        @pl.when(r == 0)
        def _():
            each_y(lambda i: rows_copy(t, h, i, 2, wait))

        @pl.when(r != 0)
        def _():
            each_y(lambda i: rows_copy(t, h, i, 1, wait))

    all_rows(0, 0, False)
    all_rows(0, 1, False)

    lsend[...] = jnp.zeros_like(lsend)
    tile = list_ref[...]
    owner = (tile * 10923) >> 16
    n = tile - owner * PER
    ox = owner >> 4
    later = jnp.where(n >= 3, 1, 0)
    q = n - 3 * later
    outer = (ox == 0) | (ox == 2)
    low = jnp.where(ox >= 2, 1, 0)
    edge0 = jnp.where(ox == 3, LATE + 5 * later, 5 * (2 * ox + later))
    edge1 = jnp.where(ox == 3, LATE + LATES[EDGE][0] + 4 * later, BASE[1] + 4 * (2 * ox + later))
    mid0 = jnp.where(outer, 16 * low + 3 * later - 2, 6 + 16 * low + 5 * later)
    mid1 = BASE[1] + jnp.where(outer, 14 * low + 3 * later - 1, 6 + 14 * low + 4 * later)
    away = outer & (q == 0)
    mid0 = jnp.where(away, LATE + 4 * low + 2 * later, mid0)
    mid1 = jnp.where(away, LATE + LATES[MID][0] + 2 * low + later, mid1)
    lsend[0:PER, 0:SEL] = tile
    start = (owner & (Z * C - 1)) * CHUNK
    for v, (b0, b1) in enumerate(((edge0, edge1), (mid0, mid1))):
        for g, (n0, n1, n2) in enumerate(((b0, b0 + 2, b1 + 2), (b0 + 1, b1 + 1, b0 + 4), (b1, b0 + 3, b1 + 3))):
            row = 8 * (1 + 3 * v + g)
            lsend[row : row + PER, 0:SEL] = start + jnp.where(q == 0, n0, jnp.where(q == 1, n1, n2))

    def list_copy(j):
        return pltpu.make_async_remote_copy(
            src_ref=lsend, dst_ref=lrecv.at[x], send_sem=l_send.at[j - 1], recv_sem=l_recv.at[j - 1],
            device_id=(blk_at((x + j) % X), y), device_id_type=MESH,
        )

    def list_arrival(j):
        return pltpu.make_async_remote_copy(
            src_ref=lsend, dst_ref=lrecv.at[(x + X - j) % X], send_sem=l_send.at[j - 1], recv_sem=l_recv.at[j - 1],
            device_id=(blk_at((x + j) % X), y), device_id_type=MESH,
        )

    def ring_copy(role, t, way, h, k, distance):
        origin = (z + (Z - distance if way == 0 else distance)) & 7
        part = region(t, origin, c, BASE[h], SIZE[role][h])
        return pltpu.make_async_remote_copy(
            src_ref=part, dst_ref=part, send_sem=ring_send.at[t, way, h, k - 1], recv_sem=ring_recv.at[t, way, h, k - 1],
            device_id=(right, left)[way], device_id_type=MESH,
        )

    def sibling(role, t, shift, h, core):
        part = region(t, (z + shift) & 7, core, BASE[h], OWN[role][h])
        return pltpu.make_async_remote_copy(
            src_ref=part, dst_ref=part, send_sem=sib_send.at[t, shift, h], recv_sem=sib_recv.at[t, shift, h],
            device_id=other, device_id_type=MESH,
        )

    def guest(t, shift, h):
        origin, count = (z + shift) & 7, (4, 2)[h]
        at = LATE + (2 * x, LATES[MID][0] + x)[h]
        return pltpu.make_async_remote_copy(
            src_ref=region(t, origin, c, BASE[h] + OWN[EDGE][h], count), dst_ref=region(t, origin, c, at, count),
            send_sem=dl_send.at[t, shift, h, 0], recv_sem=dl_recv.at[t, shift, h, x >> 1],
            device_id=(blk_at(1), y), device_id_type=MESH,
        )

    def hand_over(t, shift, h, side):
        origin, count = (z + shift) & 7, LATES[EDGE][h]
        return pltpu.make_async_remote_copy(
            src_ref=region(t, origin, c, BASE[h] + count * side, count),
            dst_ref=region(t, origin, c, LATE + (0, LATES[EDGE][0])[h], count),
            send_sem=dl_send.at[t, shift, h, side], recv_sem=dl_recv.at[t, shift, h, 0],
            device_id=(blk_at(2 * side), y), device_id_type=MESH,
        )

    def late_sibling(role, t, shift, core):
        part = region(t, (z + shift) & 7, core, LATE, sum(LATES[role]))
        return pltpu.make_async_remote_copy(
            src_ref=part, dst_ref=part, send_sem=ds_send.at[t, shift], recv_sem=ds_recv.at[t, shift],
            device_id=other, device_id_type=MESH,
        )

    def spread(role, t, shift, h):
        if role == HELP:
            for side in (0, 1):
                hand_over(t, shift, h, side).start()
            return
        sibling(role, t, shift, h, c).start()
        if role == EDGE:
            guest(t, shift, h).start()

    def late(role, t, shift):
        at = LATE
        for h in (0, 1):
            parts = (LATES[EDGE][h],) if role == EDGE else (LATES[MID][h] // 2,) * 2
            for n, count in enumerate(parts):
                part = region(t, (z + shift) & 7, c, at, count)
                pltpu.make_async_copy(part, part, dl_recv.at[t, shift, h, n]).wait()
                at += count
        late_sibling(role, t, shift, c).start()

    def own_part(role, t, h):
        part = region(t, z, c, BASE[h], SIZE[role][h])
        pltpu.make_async_copy(part, part, p1_recv.at[t, h]).wait()
        for way in (0, 1):
            ring_copy(role, t, way, h, 1, 0).start()
        spread(role, t, 0, h)

    def pass_on(role, t, h, k):
        for way in (0, 1):
            if k > HOPS[h][way]:
                continue
            ring_copy(role, t, way, h, k, k).wait_recv()
            if k < HOPS[h][way]:
                ring_copy(role, t, way, h, k + 1, k).start()
            spread(role, t, (Z - k) if way == 0 else k, h)

    def late_step(role, t, k):
        if role != HELP:
            for shift in sorted({k, (Z - k) % Z}):
                late(role, t, shift)

    def ring_sent(role, t):
        for h in (0, 1):
            for way in (0, 1):
                for k in range(1, HOPS[h][way] + 1):
                    ring_copy(role, t, way, h, k, k - 1).wait_send()
        for shift in range(Z):
            for h in (0, 1):
                if role == HELP:
                    for side in (0, 1):
                        hand_over(t, shift, h, side).wait_send()
                else:
                    sibling(role, t, shift, h, c).wait_send()
                if role == EDGE:
                    guest(t, shift, h).wait_send()
            if role != HELP:
                late_sibling(role, t, shift, c).wait_send()

    def from_sibling(role, t):
        for shift in range(Z):
            for h in (0, 1):
                sibling(role, t, shift, h, 1 - c).wait_recv()
            late_sibling(role, t, shift, 1 - c).wait_recv()

    for h in (0, 1):
        by_role(lambda role: own_part(role, 0, h))
    for j in range(1, X):
        list_copy(j).start()
    pack(1)
    all_rows(1, 0, False)
    by_role(lambda role: pass_on(role, 0, 0, 1))
    all_rows(1, 1, False)
    by_role(lambda role: pass_on(role, 0, 1, 1))
    reads[2].wait()
    each_y(lambda i: q_copy(i, False))

    def k_ring(role):
        late_step(role, 0, 0)
        for k in range(2, 4):
            for h in (0, 1):
                pass_on(role, 0, h, k)
            late_step(role, 0, k - 1)
        for h in (0, 1):
            own_part(role, 1, h)
        for h in (0, 1):
            pass_on(role, 0, h, 4)
        late_step(role, 0, 3)
        late_step(role, 0, 4)
        if role != HELP:
            from_sibling(role, 0)

    by_role(k_ring)

    def o_copy(n, src, xq, u, xh, wait):
        dst = out_ref.at[:, pl.ds(pl.multiple_of((y * HX + xh) * HD, HD), HD)]
        own = (xq == x) & (u == y)

        @pl.when(jnp.logical_not(own))
        def _():
            copy = pltpu.make_async_remote_copy(
                src_ref=src, dst_ref=dst, send_sem=o_send.at[n], recv_sem=o_recv.at[0],
                device_id=(blk_at(xq), u), device_id_type=MESH,
            )
            copy.wait_send() if wait else copy.start()

        if not wait:

            @pl.when(own)
            def _():
                pltpu.make_async_copy(src, dst, o_recv.at[0]).start()

    @pl.when(x < HX)
    def _():
        place = jnp.where(x == 1, 32, 8)
        both = (EDGE, MID)

        def cluster(i):
            return jnp.where(i < 2, 3, (x + (i >> 1)) % HX), i & 1

        def gather(i, buf):
            xq, s = cluster(i)
            for j in range(SEL):
                for g in range(GROUPS):
                    row = j * LIVE + g * 32
                    gath[row : row + 32, :] = buf[lists[xq, place + 8 * g + 3 * s, j]]
            return xq, s

        def scores(i, _):
            xq, s = gather(i, kbuf)
            lane = lax.broadcasted_iota(jnp.int32, (1, KEYS), 1)
            end = jnp.zeros((1, KEYS), jnp.int32)
            for j in range(SEL):
                end = jnp.where(lane >= j * LIVE, fill_ref[lists[xq, 3 * s, j]] + j * LIVE, end)
            bias = jnp.where(lane < end, 0.0, -1e30)
            for n in range(3):
                rows = pl.ds(pl.multiple_of(s * CROWS + n * TILE, TILE), TILE)
                sc = lax.dot_general(
                    qbuf[xq, rows, :], gath[...], (((1,), (1,)), ((), ())), preferred_element_type=jnp.float32
                )
                sc = sc + bias
                peak = jnp.max(sc, axis=1, keepdims=True)
                w = jnp.exp2((sc - peak) * C2)
                totals[i, n * TILE : (n + 1) * TILE, :] = jnp.sum(w, axis=1, keepdims=True)
                probs[i, n * TILE : (n + 1) * TILE, :] = w.astype(jnp.bfloat16)
            return 0

        def block_piece(xq, u):
            return obuf.at[xq, pl.ds(pl.multiple_of(u * PART, 32), PART)]

        relay = pltpu.make_async_remote_copy(
            src_ref=obuf.at[HX, pl.ds(0, CROWS)], dst_ref=rbuf.at[x], send_sem=r_send.at[0], recv_sem=r_recv.at[x],
            device_id=(blk_at(HX), y), device_id_type=MESH,
        )

        def mix(i, _):
            xq, s = gather(i, vbuf)
            for n in range(3):
                rows = pl.ds(pl.multiple_of(s * CROWS + n * TILE, TILE), TILE)
                o = jnp.dot(probs[i, n * TILE : (n + 1) * TILE, :], gath[...], preferred_element_type=jnp.float32)
                obuf[xq, rows, :] = (o / totals[i, n * TILE : (n + 1) * TILE, :]).astype(jnp.bfloat16)
            return xq, s

        def mix_and_send(i, _):
            xq, s = mix(i, 0)
            for w in range(4):
                o_copy(4 * i + w, block_piece(xq, 4 * s + w), xq, 4 * s + w, x, False)
            return 0

        for j in range(1, X):
            list_arrival(j).wait_recv()
        lrecv[pl.ds(x, 1)] = lsend[...][None]
        copy = pltpu.make_async_copy(lrecv, lists, l_copy.at[0])
        copy.start()
        copy.wait()
        pltpu.make_async_copy(qbuf, qbuf, q_recv.at[0]).wait()

        lax.fori_loop(0, 4, scores, 0)
        by_role(lambda role: pass_on(role, 1, 0, 1), both)
        lax.fori_loop(4, 6, scores, 0)
        by_role(lambda role: pass_on(role, 1, 1, 1), both)
        lax.fori_loop(6, 8, scores, 0)

        def v_ring(role):
            late_step(role, 1, 0)
            for k in range(2, 5):
                for h in (0, 1):
                    pass_on(role, 1, h, k)
                late_step(role, 1, k - 1)
            late_step(role, 1, 4)
            from_sibling(role, 1)

        by_role(v_ring, both)
        mix(0, 0)
        relay.start()
        lax.fori_loop(1, 8, mix_and_send, 0)

        def done(role):
            for t in (0, 1):
                ring_sent(role, t)

        by_role(done, both)
        relay.wait_send()

        def sent(i, _):
            xq, s = cluster(i)
            for w in range(4):
                o_copy(4 * i + w, block_piece(xq, 4 * s + w), xq, 4 * s + w, x, True)
            return 0

        lax.fori_loop(1, 8, sent, 0)

    @pl.when(x == HX)
    def _():
        for k in range(1, 5):
            for h in (0, 1):
                pass_on(HELP, 1, h, k)
        for j in range(1, X):
            list_arrival(j).wait_recv()
        for t in (0, 1):
            ring_sent(HELP, t)

        def column(wait):
            for xh in range(HX):
                if not wait:
                    pltpu.make_async_copy(rbuf.at[xh], rbuf.at[xh], r_recv.at[xh]).wait()
                for w in range(4):
                    o_copy(4 * xh + w, rbuf.at[xh, pl.ds(w * PART, PART)], x, w, xh, wait)

        column(False)
        column(True)

    for t in (0, 1):
        for h in (0, 1):
            all_rows(t, h, True)
    each_y(lambda i: q_copy(i, True))
    for j in range(1, X):
        list_copy(j).wait_send()
    pltpu.make_async_copy(out_ref, out_ref, o_recv.at[0]).wait()


def local(queries, keys, values, key_lists, key_fill):
    bf = jnp.bfloat16
    anywhere = pl.BlockSpec(memory_space=pl.ANY)
    dma = pltpu.SemaphoreType.DMA
    return pl.pallas_call(
        kernel,
        out_shape=jax.ShapeDtypeStruct(queries.shape, bf),
        in_specs=[
            anywhere, anywhere, anywhere,
            pl.BlockSpec(memory_space=pltpu.VMEM), pl.BlockSpec(memory_space=pltpu.SMEM),
        ],
        out_specs=anywhere,
        scratch_shapes=[
            pltpu.VMEM((PART, HEADS * HD), bf),
            pltpu.VMEM((PART, HEADS * HD), bf),
            pltpu.VMEM((PART, HEADS * HD), bf),
            pltpu.VMEM((HEADS, GROUPS, 32, HD), bf),
            pltpu.VMEM((HEADS, GROUPS, 32, HD), bf),
            pltpu.VMEM((Z * C * CHUNK, 32, HD), bf),
            pltpu.VMEM((Z * C * CHUNK, 32, HD), bf),
            pltpu.VMEM((X, BLOCK, HD), bf),
            pltpu.VMEM((X, BLOCK, HD), bf),
            pltpu.VMEM((HX, CROWS, HD), bf),
            pltpu.VMEM((KEYS, HD), bf),
            pltpu.VMEM((2 * X, CROWS, KEYS), bf),
            pltpu.VMEM((2 * X, CROWS, 1), jnp.float32),
            pltpu.VMEM((56, 128), jnp.int32),
            pltpu.VMEM((X, 56, 128), jnp.int32),
            pltpu.SMEM((X, 56, 128), jnp.int32),
            dma((3,)),
            dma((5, HEADS)),
            dma((2, 2)),
            dma((1,)),
            dma((2, 2, 2, 4)),
            dma((2, 2, 2, 4)),
            dma((2, Z, 2)),
            dma((2, Z, 2)),
            dma((2, Z, 2, 2)),
            dma((2, Z, 2, 2)),
            dma((2, Z)),
            dma((2, Z)),
            dma((X - 1,)),
            dma((X - 1,)),
            dma((1,)),
            dma((X * Y,)),
            dma((1,)),
            dma((1,)),
            dma((HX,)),
        ],
        compiler_params=pltpu.CompilerParams(
            collective_id=0, has_side_effects=True, vmem_limit_bytes=56 * 1024 * 1024
        ),
        cost_estimate=pl.CostEstimate(flops=5_000_000_000, bytes_accessed=4_000_000, transcendentals=4_800_000),
    )(queries, keys, values, key_lists, key_fill)


def solution(mesh):
    in_specs = (
        P(("blk", "uly"), None),
        P(("blk", "uly"), None),
        P(("blk", "uly"), None),
        P("blk", None),
        P(),
    )
    out_specs = P(("blk", "uly"), None)
    return jax.shard_map(local, mesh=mesh, in_specs=in_specs, out_specs=out_specs, check_vma=False)
```

```python
import math

import jax
import jax.numpy as jnp
from jax import lax
from jax.experimental import pallas as pl
from jax.experimental.pallas import tpu as pltpu
from jax.sharding import PartitionSpec as P

HD = 128
TILE = 128
SEL = 16
LIVE = 96
X, Z, C, Y = 4, 8, 2, 8
HX = 3
HEADS = HX * Y
PART = 96
BLOCK = PART * Y
PER = BLOCK // TILE
CROWS = BLOCK // 2
KEYS = SEL * LIVE
GROUPS = LIVE // 32
SLOTS = 26
CHUNK = SLOTS * GROUPS
LATE = 20 * GROUPS
GUEST = 18 * GROUPS
EDGE, MID, HELP = 0, 1, 2
PARTS = {EDGE: ((2, 54, 6), (0, 0, 30), (1, 30, 24)), MID: ((0, 0, 30), (1, 30, 30)), HELP: ((0, 0, 18), (1, 18, 18))}
HOPS = ((4, 3), (3, 4), (3, 4))
MESH = pl.DeviceIdType.MESH
C2 = math.log2(math.e) / math.sqrt(HD)


def kernel(
    q_ref, k_ref, v_ref, list_ref, fill_ref, out_ref,
    qin, kin, vin, kpack, vpack, kbuf, vbuf, qbuf, obuf, gath, probs, totals, lsend, lrecv, lists,
    in_sem, p1_send, p1_recv, q_recv, ring_send, ring_recv, sib_send, sib_recv, dl_send, dl_recv, ds_send, ds_recv,
    l_send, l_recv, l_copy, o_send, o_recv,
):
    blk, y = lax.axis_index("blk"), lax.axis_index("uly")
    x, z, c = blk >> 4, (blk >> 1) & 7, blk & 1
    plane = blk & 15
    r, a = y & 3, y >> 2
    role_of = ((x & 1) == 0, x == 1, x == 3)

    def by_role(f, roles=(EDGE, MID, HELP)):
        for role in roles:
            pl.when(role_of[role])(lambda role=role: f(role))

    reads = [
        pltpu.make_async_copy(src, dst, in_sem.at[n])
        for n, (src, dst) in enumerate(((k_ref, kin), (v_ref, vin), (q_ref, qin)))
    ]
    for copy in reads:
        copy.start()

    def blk_at(xx):
        return (xx << 4) + plane

    barrier = pltpu.get_barrier_semaphore()
    right = ((blk & 49) + (((z + 1) & 7) << 1), y)
    left = ((blk & 49) + (((z + 7) & 7) << 1), y)
    other = (blk ^ 1, y)
    near = [(blk_at((x + i) & 3), (y + j) & 7) for j in range(Y) for i in range(X) if i or j]
    for d in (right, left, other, *near):
        pl.semaphore_signal(barrier, inc=1, device_id=d, device_id_type=MESH)

    lsend[...] = jnp.zeros_like(lsend)
    tile = list_ref[...]
    owner = (tile * 10923) >> 16
    n = tile - owner * PER
    ox = owner >> 4
    start = (owner & (Z * C - 1)) * SLOTS
    edge = ox * PER + n + jnp.where(ox == 3, 2, 0)
    first = (n == 0) | (n == 3)
    outer = jnp.where(first, 20 + ox + jnp.where(n == 3, 1, 0), ox * 5 + n - 1 - jnp.where(n > 3, 1, 0))
    inner = jnp.where(ox == 1, 4, 14) + n
    middle = jnp.where((ox == 0) | (ox == 2), outer, inner)
    lsend[0:PER, 0:SEL] = tile
    lsend[8 : 8 + PER, 0:SEL] = (start + edge) * GROUPS
    lsend[16 : 16 + PER, 0:SEL] = (start + middle) * GROUPS

    piece0 = pl.multiple_of(jnp.where(r == 1, 32, 0), 32)
    piece1 = pl.multiple_of(jnp.where((r == 1) | (r == 2), 64, 32), 32)

    def pack(t):
        src, dst = ((kin, kpack), (vin, vpack))[t]
        reads[t].wait()
        for h in range(HEADS):
            cols = slice(h * HD, (h + 1) * HD)
            dst[h, 0] = src[pl.ds(piece0, 32), cols]
            dst[h, 1] = src[pl.ds(piece1, 32), cols]
            dst[h, 2] = src[64:96, cols]

    pack(0)
    pl.semaphore_wait(barrier, len(near) + 3)

    bufs = (kbuf, vbuf)

    def region(t, zz, core, at, count):
        return bufs[t].at[pl.ds((zz * C + core) * CHUNK + at, count)]

    off = jnp.where(r == 0, 0, 1 + 2 * r)
    wing = (x == 0) | (x == 2)
    i32 = jnp.int32

    def target(xh):
        if xh != 1:
            helped = x == 3
            xd = jnp.where(helped, 3, xh)
            at = jnp.where(helped, (PER if xh else 0), x * PER) * GROUPS + 9 * a + off
            half = jnp.where(helped, xh // 2, jnp.where((x == 2) | ((x == 1) & (a == 1) & (r != 0)), 1, 0))
            return xd, at, half
        guest = wing & (r == 0)
        xd = jnp.where(guest, x, 1)
        own = jnp.where(wing, 5 * x * GROUPS + 6 * a + off - 3, jnp.where(x == 1, 4, 14) * GROUPS + 9 * a + off)
        at = jnp.where(guest, GUEST + GROUPS * a, own)
        half = jnp.where(guest, 2, jnp.where(x >= 2, 1, 0))
        return xd, at, half

    targets = [target(xh) for xh in range(HX)]

    def rows_copy(t, i, rows, wait):
        yh = (y + 4 + i) & 7
        for xh, (xd, at, half) in enumerate(targets):
            own = (xd == x) & (yh == y)
            src = (kpack, vpack)[t].at[yh * HX + xh, pl.ds(0, rows)]
            dst = region(t, z, c, at, rows)

            @pl.when(jnp.logical_not(own))
            def _():
                copy = pltpu.make_async_remote_copy(
                    src_ref=src, dst_ref=dst, send_sem=p1_send.at[t, i * HX + xh], recv_sem=p1_recv.at[t, half],
                    device_id=(blk_at(xd), yh), device_id_type=MESH,
                )
                copy.wait_send() if wait else copy.start()

            if not wait:

                @pl.when(own)
                def _():
                    pltpu.make_async_copy(src, dst, p1_recv.at[t, half]).start()

    def q_copy(i, wait):
        yh = (y + 4 + i) & 7
        for xh in range(HX):
            own = (xh == x) & (yh == y)
            src = qin.at[:, pl.ds(pl.multiple_of((yh * HX + xh) * HD, HD), HD)]
            dst = qbuf.at[x, pl.ds(pl.multiple_of(y * PART, 32), PART)]

            @pl.when(jnp.logical_not(own))
            def _():
                copy = pltpu.make_async_remote_copy(
                    src_ref=src, dst_ref=dst, send_sem=p1_send.at[2, i * HX + xh], recv_sem=q_recv.at[0],
                    device_id=(blk_at(xh), yh), device_id_type=MESH,
                )
                copy.wait_send() if wait else copy.start()

            if not wait:

                @pl.when(own)
                def _():
                    pltpu.make_async_copy(src, dst, q_recv.at[0]).start()

    def each_y(body):
        def step(i, _):
            body(i)
            return 0

        lax.fori_loop(0, Y, step, 0)

    def all_rows(t, wait):
        @pl.when(r == 0)
        def _():
            each_y(lambda i: rows_copy(t, i, 3, wait))

        @pl.when(r != 0)
        def _():
            each_y(lambda i: rows_copy(t, i, 2, wait))

    all_rows(0, False)

    def list_copy(j):
        return pltpu.make_async_remote_copy(
            src_ref=lsend, dst_ref=lrecv.at[x], send_sem=l_send.at[j - 1], recv_sem=l_recv.at[j - 1],
            device_id=(blk_at((x + j) % X), y), device_id_type=MESH,
        )

    def list_arrival(j):
        return pltpu.make_async_remote_copy(
            src_ref=lsend, dst_ref=lrecv.at[(x + X - j) % X], send_sem=l_send.at[j - 1], recv_sem=l_recv.at[j - 1],
            device_id=(blk_at((x + j) % X), y), device_id_type=MESH,
        )

    for j in range(1, X):
        list_copy(j).start()

    def ring_copy(t, way, part, k, distance):
        n, at, size = part
        origin = (z + (Z - distance if way == 0 else distance)) & 7
        rows = region(t, origin, c, at, size)
        return pltpu.make_async_remote_copy(
            src_ref=rows, dst_ref=rows, send_sem=ring_send.at[t, way, n, k - 1], recv_sem=ring_recv.at[t, way, n, k - 1],
            device_id=(right, left)[way], device_id_type=MESH,
        )

    def sibling(t, shift, part, core):
        n, at, size = part
        rows = region(t, (z + shift) & 7, core, at, size)
        return pltpu.make_async_remote_copy(
            src_ref=rows, dst_ref=rows, send_sem=sib_send.at[t, shift, n], recv_sem=sib_recv.at[t, shift, n],
            device_id=other, device_id_type=MESH,
        )

    def guest(t, shift):
        origin = (z + shift) & 7
        return pltpu.make_async_remote_copy(
            src_ref=region(t, origin, c, GUEST, 2 * GROUPS), dst_ref=region(t, origin, c, LATE + GROUPS * x, 2 * GROUPS),
            send_sem=dl_send.at[t, shift, 0], recv_sem=dl_recv.at[t, shift, x >> 1],
            device_id=(blk_at(1), y), device_id_type=MESH,
        )

    def hand_over(t, shift, part):
        n, at, size = part
        origin = (z + shift) & 7
        return pltpu.make_async_remote_copy(
            src_ref=region(t, origin, c, at, size), dst_ref=region(t, origin, c, LATE, size),
            send_sem=dl_send.at[t, shift, n], recv_sem=dl_recv.at[t, shift, 0],
            device_id=(blk_at(2 * n), y), device_id_type=MESH,
        )

    def late_sibling(role, t, shift, core):
        rows = region(t, (z + shift) & 7, core, LATE, (18, 12)[role])
        return pltpu.make_async_remote_copy(
            src_ref=rows, dst_ref=rows, send_sem=ds_send.at[t, shift], recv_sem=ds_recv.at[t, shift],
            device_id=other, device_id_type=MESH,
        )

    def spread(role, t, shift, part):
        if role == HELP:
            hand_over(t, shift, part).start()
        elif part[0] == 2:
            guest(t, shift).start()
        else:
            sibling(t, shift, part, c).start()

    def late(role, t, shift):
        size = (18, 6)[role]
        for n in range((1, 2)[role]):
            rows = region(t, (z + shift) & 7, c, LATE + size * n, size)
            pltpu.make_async_copy(rows, rows, dl_recv.at[t, shift, n]).wait()
        late_sibling(role, t, shift, c).start()

    def late_pair(role, t, k):
        late(role, t, k)
        late(role, t, Z - k)

    def own_part(role, t):
        for part in PARTS[role]:
            n, at, size = part
            rows = region(t, z, c, at, size)
            pltpu.make_async_copy(rows, rows, p1_recv.at[t, n]).wait()
            for way in (0, 1):
                ring_copy(t, way, part, 1, 0).start()
            spread(role, t, 0, part)

    def pass_on(role, t, k, parts=(0, 1, 2)):
        for part in PARTS[role]:
            n = part[0]
            if n not in parts:
                continue
            for way in (0, 1):
                last = HOPS[n][way]
                if isinstance(k, int) and k > last:
                    continue
                ring_copy(t, way, part, k, k).wait_recv()
                if isinstance(k, int):
                    if k < last:
                        ring_copy(t, way, part, k + 1, k).start()
                elif last == 4:
                    ring_copy(t, way, part, k + 1, k).start()
                else:

                    @pl.when(k < last)
                    def _():
                        ring_copy(t, way, part, k + 1, k).start()

                spread(role, t, (Z - k) if way == 0 else k, part)

    def ring_sent(role, t):
        for part in PARTS[role]:
            for way in (0, 1):
                for k in range(1, HOPS[part[0]][way] + 1):
                    ring_copy(t, way, part, k, k - 1).wait_send()
            for shift in range(Z):
                if role == HELP:
                    hand_over(t, shift, part).wait_send()
                elif part[0] == 2:
                    guest(t, shift).wait_send()
                else:
                    sibling(t, shift, part, c).wait_send()
        if role != HELP:
            for shift in range(Z):
                late_sibling(role, t, shift, c).wait_send()

    def from_sibling(role, t):
        for shift in range(Z):
            for part in PARTS[role]:
                if part[0] < 2:
                    sibling(t, shift, part, 1 - c).wait_recv()
            late_sibling(role, t, shift, 1 - c).wait_recv()

    by_role(lambda role: own_part(role, 0))
    pack(1)
    all_rows(1, False)
    by_role(lambda role: pass_on(role, 0, 1, (0, 2)))
    reads[2].wait()
    each_y(lambda i: q_copy(i, False))
    by_role(lambda role: pass_on(role, 0, 1, (1,)))

    def k_ring(role):
        if role != HELP:
            late(role, 0, 0)
        for k in (2, 3):
            pass_on(role, 0, k)
            if role != HELP:
                late_pair(role, 0, k - 1)
        own_part(role, 1)
        pass_on(role, 0, 4)
        if role != HELP:
            late_pair(role, 0, 3)
            late(role, 0, 4)
            from_sibling(role, 0)

    by_role(k_ring)

    def o_copy(n, src, xq, u, xh, wait):
        dst = out_ref.at[:, pl.ds(pl.multiple_of((y * HX + xh) * HD, HD), HD)]
        own = (xq == x) & (u == y)

        @pl.when(jnp.logical_not(own))
        def _():
            copy = pltpu.make_async_remote_copy(
                src_ref=src, dst_ref=dst, send_sem=o_send.at[n], recv_sem=o_recv.at[0],
                device_id=(blk_at(xq), u), device_id_type=MESH,
            )
            copy.wait_send() if wait else copy.start()

        if not wait:

            @pl.when(own)
            def _():
                pltpu.make_async_copy(src, dst, o_recv.at[0]).start()

    @pl.when(x < HX)
    def _():
        place = jnp.where(x == 1, 16, 8)
        both = (EDGE, MID)

        def cluster(i):
            return (x + 1 + (i >> 1)) & 3, i & 1

        def gather(i, buf):
            xq, s = cluster(i)
            for j in range(SEL):
                at = lists[xq, place + 3 * s, j]
                gath[j * LIVE : (j + 1) * LIVE, :] = buf[pl.ds(at, GROUPS)].reshape(LIVE, HD)
            return xq, s

        def scores(i, _):
            xq, s = gather(i, kbuf)
            lane = lax.broadcasted_iota(jnp.int32, (1, KEYS), 1)
            end = jnp.zeros((1, KEYS), jnp.int32)
            for j in range(SEL):
                end = jnp.where(lane >= j * LIVE, fill_ref[lists[xq, 3 * s, j]] + j * LIVE, end)
            bias = jnp.where(lane < end, 0.0, -1e30)
            for n in range(3):
                rows = pl.ds(pl.multiple_of(s * CROWS + n * TILE, TILE), TILE)
                sc = lax.dot_general(
                    qbuf[xq, rows, :], gath[...], (((1,), (1,)), ((), ())), preferred_element_type=jnp.float32
                )
                sc = sc + bias
                peak = jnp.max(sc, axis=1, keepdims=True)
                w = jnp.exp2((sc - peak) * C2)
                totals[i, n * TILE : (n + 1) * TILE, :] = jnp.sum(w, axis=1, keepdims=True)
                probs[i, n * TILE : (n + 1) * TILE, :] = w.astype(jnp.bfloat16)
            return 0

        def block_piece(xq, u):
            return obuf.at[xq, pl.ds(pl.multiple_of(u * PART, 32), PART)]

        def mix(i, _):
            xq, s = gather(i, vbuf)
            for n in range(3):
                rows = pl.ds(pl.multiple_of(s * CROWS + n * TILE, TILE), TILE)
                o = jnp.dot(probs[i, n * TILE : (n + 1) * TILE, :], gath[...], preferred_element_type=jnp.float32)
                obuf[xq, rows, :] = (o / totals[i, n * TILE : (n + 1) * TILE, :]).astype(jnp.bfloat16)
            for w in range(4):
                o_copy(4 * i + w, block_piece(xq, 4 * s + w), xq, 4 * s + w, x, False)
            return 0

        for j in range(1, X):
            list_arrival(j).wait_recv()
        lrecv[pl.ds(x, 1)] = lsend[...][None]
        copy = pltpu.make_async_copy(lrecv, lists, l_copy.at[0])
        copy.start()
        copy.wait()
        pltpu.make_async_copy(qbuf, qbuf, q_recv.at[0]).wait()

        by_role(lambda role: late(role, 1, 0), both)

        def v_step(k, _):
            by_role(lambda role: pass_on(role, 1, k, (0, 2)), both)
            scores(2 * k - 2, 0)
            by_role(lambda role: pass_on(role, 1, k, (1,)), both)
            scores(2 * k - 1, 0)

            @pl.when(k > 1)
            def _():
                by_role(lambda role: late_pair(role, 1, k - 1), both)

            return 0

        lax.fori_loop(1, 4, v_step, 0)
        lax.fori_loop(6, 8, scores, 0)

        def v_end(role):
            late_pair(role, 1, 3)
            pass_on(role, 1, 4)
            late(role, 1, 4)
            from_sibling(role, 1)

        by_role(v_end, both)
        lax.fori_loop(0, 8, mix, 0)

        def done(role):
            for t in (0, 1):
                ring_sent(role, t)

        by_role(done, both)

        def sent(i, _):
            xq, s = cluster(i)
            for w in range(4):
                o_copy(4 * i + w, block_piece(xq, 4 * s + w), xq, 4 * s + w, x, True)
            return 0

        lax.fori_loop(0, 8, sent, 0)

    @pl.when(x == HX)
    def _():
        for k in range(1, 5):
            pass_on(HELP, 1, k)
        for j in range(1, X):
            list_arrival(j).wait_recv()
        for t in (0, 1):
            ring_sent(HELP, t)

    all_rows(0, True)
    all_rows(1, True)
    each_y(lambda i: q_copy(i, True))
    for j in range(1, X):
        list_copy(j).wait_send()
    pltpu.make_async_copy(out_ref, out_ref, o_recv.at[0]).wait()


def local(queries, keys, values, key_lists, key_fill):
    bf = jnp.bfloat16
    anywhere = pl.BlockSpec(memory_space=pl.ANY)
    dma = pltpu.SemaphoreType.DMA
    return pl.pallas_call(
        kernel,
        out_shape=jax.ShapeDtypeStruct(queries.shape, bf),
        in_specs=[
            anywhere, anywhere, anywhere,
            pl.BlockSpec(memory_space=pltpu.VMEM), pl.BlockSpec(memory_space=pltpu.SMEM),
        ],
        out_specs=anywhere,
        scratch_shapes=[
            pltpu.VMEM((PART, HEADS * HD), bf),
            pltpu.VMEM((PART, HEADS * HD), bf),
            pltpu.VMEM((PART, HEADS * HD), bf),
            pltpu.VMEM((HEADS, GROUPS, 32, HD), bf),
            pltpu.VMEM((HEADS, GROUPS, 32, HD), bf),
            pltpu.VMEM((Z * C * CHUNK, 32, HD), bf),
            pltpu.VMEM((Z * C * CHUNK, 32, HD), bf),
            pltpu.VMEM((X, BLOCK, HD), bf),
            pltpu.VMEM((X, BLOCK, HD), bf),
            pltpu.VMEM((KEYS, HD), bf),
            pltpu.VMEM((2 * X, CROWS, KEYS), bf),
            pltpu.VMEM((2 * X, CROWS, 1), jnp.float32),
            pltpu.VMEM((24, 128), jnp.int32),
            pltpu.VMEM((X, 24, 128), jnp.int32),
            pltpu.SMEM((X, 24, 128), jnp.int32),
            dma((3,)),
            dma((3, HEADS)),
            dma((2, 3)),
            dma((1,)),
            dma((2, 2, 3, 4)),
            dma((2, 2, 3, 4)),
            dma((2, Z, 2)),
            dma((2, Z, 2)),
            dma((2, Z, 2)),
            dma((2, Z, 2)),
            dma((2, Z)),
            dma((2, Z)),
            dma((X - 1,)),
            dma((X - 1,)),
            dma((1,)),
            dma((X * Y,)),
            dma((1,)),
        ],
        compiler_params=pltpu.CompilerParams(
            collective_id=0, has_side_effects=True, vmem_limit_bytes=56 * 1024 * 1024
        ),
        cost_estimate=pl.CostEstimate(flops=5_000_000_000, bytes_accessed=4_000_000, transcendentals=4_800_000),
    )(queries, keys, values, key_lists, key_fill)


def solution(mesh):
    in_specs = (
        P(("blk", "uly"), None),
        P(("blk", "uly"), None),
        P(("blk", "uly"), None),
        P("blk", None),
        P(),
    )
    out_specs = P(("blk", "uly"), None)
    return jax.shard_map(local, mesh=mesh, in_specs=in_specs, out_specs=out_specs, check_vma=False)
```

```python
import math

import jax
import jax.numpy as jnp
from jax import lax
from jax.experimental import pallas as pl
from jax.experimental.pallas import tpu as pltpu
from jax.sharding import PartitionSpec as P

HD = 128
TILE = 128
SEL = 16
LIVE = 96
X, Z, C, Y = 4, 8, 2, 8
HX = 3
HEADS = HX * Y
PART = 96
BLOCK = PART * Y
PER = BLOCK // TILE
CROWS = BLOCK // 2
KEYS = SEL * LIVE
GROUPS = LIVE // 32
SLOTS = 26
CHUNK = SLOTS * GROUPS
LATE = 20 * GROUPS
GUEST = 18 * GROUPS
EDGE, MID, HELP = 0, 1, 2
PARTS = {EDGE: ((2, 54, 6), (0, 0, 30), (1, 30, 24)), MID: ((0, 0, 30), (1, 30, 30)), HELP: ((0, 0, 18), (1, 18, 18))}
HOPS = ((4, 3), (3, 4), (3, 4))
MESH = pl.DeviceIdType.MESH
C2 = math.log2(math.e) / math.sqrt(HD)


def kernel(
    q_ref, k_ref, v_ref, list_ref, fill_ref, out_ref,
    qin, kin, vin, kpack, vpack0, vpack1, kbuf, vbuf0, vbuf1, qbuf, obuf, oin, gath, probs, totals, lsend, lrecv, lists,
    in_sem, p1_send, p1_recv, q_recv, ring_send, ring_recv, sib_send, sib_recv, dl_send, dl_recv, ds_send, ds_recv,
    l_send, l_recv, l_copy, o_send, o_recv,
):
    blk, y = lax.axis_index("blk"), lax.axis_index("uly")
    x, z, c = blk >> 4, (blk >> 1) & 7, blk & 1
    plane = blk & 15
    r, a = y & 3, y >> 2
    role_of = ((x & 1) == 0, x == 1, x == 3)

    def by_role(f, roles=(EDGE, MID, HELP)):
        for role in roles:
            pl.when(role_of[role])(lambda role=role: f(role))

    reads = [
        pltpu.make_async_copy(src, dst, in_sem.at[n])
        for n, (src, dst) in enumerate(((k_ref, kin), (v_ref, vin), (q_ref, qin)))
    ]
    for copy in reads:
        copy.start()

    def blk_at(xx):
        return (xx << 4) + plane

    barrier = pltpu.get_barrier_semaphore()
    right = ((blk & 49) + (((z + 1) & 7) << 1), y)
    left = ((blk & 49) + (((z + 7) & 7) << 1), y)
    other = (blk ^ 1, y)
    near = [(blk_at((x + i) & 3), (y + j) & 7) for j in range(Y) for i in range(X) if i or j]
    for d in (right, left, other, *near):
        pl.semaphore_signal(barrier, inc=1, device_id=d, device_id_type=MESH)

    lsend[...] = jnp.zeros_like(lsend)
    tile = list_ref[...]
    owner = (tile * 10923) >> 16
    n = tile - owner * PER
    ox = owner >> 4
    start = (owner & (Z * C - 1)) * SLOTS
    edge = ox * PER + n + jnp.where(ox == 3, 2, 0)
    first = (n == 0) | (n == 3)
    outer = jnp.where(first, 20 + ox + jnp.where(n == 3, 1, 0), ox * 5 + n - 1 - jnp.where(n > 3, 1, 0))
    inner = jnp.where(ox == 1, 4, 14) + n
    middle = jnp.where((ox == 0) | (ox == 2), outer, inner)
    lsend[0:PER, 0:SEL] = tile
    lsend[8 : 8 + PER, 0:SEL] = (start + edge) * GROUPS
    lsend[16 : 16 + PER, 0:SEL] = (start + middle) * GROUPS

    piece0 = pl.multiple_of(jnp.where(r == 1, 32, 0), 32)
    piece1 = pl.multiple_of(jnp.where((r == 1) | (r == 2), 64, 32), 32)

    def pieces(src, h):
        cols = slice(h * HD, (h + 1) * HD)
        return src[pl.ds(piece0, 32), cols], src[pl.ds(piece1, 32), cols], src[64:96, cols]

    def pack_k():
        reads[0].wait()
        for h in range(HEADS):
            for g, rows in enumerate(pieces(kin, h)):
                kpack[h, g] = rows

    def paired(top, bottom):
        left = lax.broadcasted_iota(jnp.int32, top.shape, 1) < HD // 2
        return (
            jnp.where(left, top, pltpu.roll(bottom, HD // 2, 1)).astype(jnp.bfloat16),
            jnp.where(left, pltpu.roll(top, HD // 2, 1), bottom).astype(jnp.bfloat16),
        )

    def pack_v():
        reads[1].wait()
        for h in range(HEADS):
            for g, rows in enumerate(pieces(vin, h)):
                rows = rows.astype(jnp.float32)
                vpack0[h, g], vpack1[h, g] = paired(rows[0:16], rows[16:32])

    pack_k()
    pl.semaphore_wait(barrier, len(near) + 3)

    bufs = (kbuf, vbuf0, vbuf1)

    def region(t, zz, core, at, count):
        return bufs[t].at[pl.ds((zz * C + core) * CHUNK + at, count)]

    off = jnp.where(r == 0, 0, 1 + 2 * r)
    wing = (x == 0) | (x == 2)
    i32 = jnp.int32

    def target(xh):
        if xh != 1:
            helped = x == 3
            xd = jnp.where(helped, 3, xh)
            at = jnp.where(helped, (PER if xh else 0), x * PER) * GROUPS + 9 * a + off
            half = jnp.where(helped, xh // 2, jnp.where((x == 2) | ((x == 1) & (a == 1) & (r != 0)), 1, 0))
            return xd, at, half
        guest = wing & (r == 0)
        xd = jnp.where(guest, x, 1)
        own = jnp.where(wing, 5 * x * GROUPS + 6 * a + off - 3, jnp.where(x == 1, 4, 14) * GROUPS + 9 * a + off)
        at = jnp.where(guest, GUEST + GROUPS * a, own)
        half = jnp.where(guest, 2, jnp.where(x >= 2, 1, 0))
        return xd, at, half

    targets = [target(xh) for xh in range(HX)]

    def rows_copy(t, i, rows, wait):
        yh = (y + 4 + i) & 7
        for xh, (xd, at, half) in enumerate(targets):
            own = (xd == x) & (yh == y)
            src = (kpack, vpack0, vpack1)[t].at[yh * HX + xh, pl.ds(0, rows)]
            dst = region(t, z, c, at, rows)

            @pl.when(jnp.logical_not(own))
            def _():
                copy = pltpu.make_async_remote_copy(
                    src_ref=src, dst_ref=dst, send_sem=p1_send.at[t, i * HX + xh], recv_sem=p1_recv.at[t, half],
                    device_id=(blk_at(xd), yh), device_id_type=MESH,
                )
                copy.wait_send() if wait else copy.start()

            if not wait:

                @pl.when(own)
                def _():
                    pltpu.make_async_copy(src, dst, p1_recv.at[t, half]).start()

    def q_copy(i, wait):
        yh = (y + 4 + i) & 7
        for xh in range(HX):
            own = (xh == x) & (yh == y)
            src = qin.at[:, pl.ds(pl.multiple_of((yh * HX + xh) * HD, HD), HD)]
            dst = qbuf.at[x, pl.ds(pl.multiple_of(y * PART, 32), PART)]

            @pl.when(jnp.logical_not(own))
            def _():
                copy = pltpu.make_async_remote_copy(
                    src_ref=src, dst_ref=dst, send_sem=p1_send.at[3, i * HX + xh], recv_sem=q_recv.at[0],
                    device_id=(blk_at(xh), yh), device_id_type=MESH,
                )
                copy.wait_send() if wait else copy.start()

            if not wait:

                @pl.when(own)
                def _():
                    pltpu.make_async_copy(src, dst, q_recv.at[0]).start()

    def each_y(body):
        def step(i, _):
            body(i)
            return 0

        lax.fori_loop(0, Y, step, 0)

    def all_rows(t, wait):
        @pl.when(r == 0)
        def _():
            each_y(lambda i: rows_copy(t, i, 3, wait))

        @pl.when(r != 0)
        def _():
            each_y(lambda i: rows_copy(t, i, 2, wait))

    all_rows(0, False)

    def list_copy(j):
        return pltpu.make_async_remote_copy(
            src_ref=lsend, dst_ref=lrecv.at[x], send_sem=l_send.at[j - 1], recv_sem=l_recv.at[j - 1],
            device_id=(blk_at((x + j) % X), y), device_id_type=MESH,
        )

    def list_arrival(j):
        return pltpu.make_async_remote_copy(
            src_ref=lsend, dst_ref=lrecv.at[(x + X - j) % X], send_sem=l_send.at[j - 1], recv_sem=l_recv.at[j - 1],
            device_id=(blk_at((x + j) % X), y), device_id_type=MESH,
        )

    for j in range(1, X):
        list_copy(j).start()

    def ring_copy(t, way, part, k, distance):
        n, at, size = part
        origin = (z + (Z - distance if way == 0 else distance)) & 7
        rows = region(t, origin, c, at, size)
        return pltpu.make_async_remote_copy(
            src_ref=rows, dst_ref=rows, send_sem=ring_send.at[t], recv_sem=ring_recv.at[t, way, n, k - 1],
            device_id=(right, left)[way], device_id_type=MESH,
        )

    def sibling(t, shift, part, core):
        n, at, size = part
        rows = region(t, (z + shift) & 7, core, at, size)
        return pltpu.make_async_remote_copy(
            src_ref=rows, dst_ref=rows, send_sem=sib_send.at[t], recv_sem=sib_recv.at[t, shift, n],
            device_id=other, device_id_type=MESH,
        )

    def guest(t, shift):
        origin = (z + shift) & 7
        return pltpu.make_async_remote_copy(
            src_ref=region(t, origin, c, GUEST, 2 * GROUPS), dst_ref=region(t, origin, c, LATE + GROUPS * x, 2 * GROUPS),
            send_sem=dl_send.at[t], recv_sem=dl_recv.at[t, shift, x >> 1],
            device_id=(blk_at(1), y), device_id_type=MESH,
        )

    def hand_over(t, shift, part):
        n, at, size = part
        origin = (z + shift) & 7
        return pltpu.make_async_remote_copy(
            src_ref=region(t, origin, c, at, size), dst_ref=region(t, origin, c, LATE, size),
            send_sem=dl_send.at[t], recv_sem=dl_recv.at[t, shift, 0],
            device_id=(blk_at(2 * n), y), device_id_type=MESH,
        )

    def late_sibling(role, t, shift, core):
        rows = region(t, (z + shift) & 7, core, LATE, (18, 12)[role])
        return pltpu.make_async_remote_copy(
            src_ref=rows, dst_ref=rows, send_sem=ds_send.at[t], recv_sem=ds_recv.at[t, shift],
            device_id=other, device_id_type=MESH,
        )

    def spread(role, t, shift, part):
        if role == HELP:
            hand_over(t, shift, part).start()
        elif part[0] == 2:
            guest(t, shift).start()
        else:
            sibling(t, shift, part, c).start()

    def late(role, t, shift):
        size = (18, 6)[role]
        for n in range((1, 2)[role]):
            rows = region(t, (z + shift) & 7, c, LATE + size * n, size)
            pltpu.make_async_copy(rows, rows, dl_recv.at[t, shift, n]).wait()
        late_sibling(role, t, shift, c).start()

    def late_pair(role, t, k):
        late(role, t, k)
        late(role, t, Z - k)

    def own_part(role, t):
        for part in PARTS[role]:
            n, at, size = part
            rows = region(t, z, c, at, size)
            pltpu.make_async_copy(rows, rows, p1_recv.at[t, n]).wait()
            for way in (0, 1):
                ring_copy(t, way, part, 1, 0).start()
            spread(role, t, 0, part)

    def pass_on(role, t, k, parts=(0, 1, 2)):
        for part in PARTS[role]:
            n = part[0]
            if n not in parts:
                continue
            for way in (0, 1):
                last = HOPS[n][way]
                if isinstance(k, int) and k > last:
                    continue
                ring_copy(t, way, part, k, k).wait_recv()
                if isinstance(k, int):
                    if k < last:
                        ring_copy(t, way, part, k + 1, k).start()
                elif last == 4:
                    ring_copy(t, way, part, k + 1, k).start()
                else:

                    @pl.when(k < last)
                    def _():
                        ring_copy(t, way, part, k + 1, k).start()

                spread(role, t, (Z - k) if way == 0 else k, part)

    def sent_all(t, sem, groups):
        rows = bufs[t].at[pl.ds(0, groups)]
        pltpu.make_async_copy(rows, rows, sem.at[t]).wait()

    def ring_sent(role, t):
        sizes = [size for n, _, size in PARTS[role] if n < 2]
        guests = 6 if role == EDGE else 0
        sent_all(t, ring_send, (sum(sizes) + guests) * (Z - 1))
        if role == HELP:
            sent_all(t, dl_send, sum(sizes) * Z)
            return
        sent_all(t, sib_send, sum(sizes) * Z)
        sent_all(t, ds_send, (18, 12)[role] * Z)
        if guests:
            sent_all(t, dl_send, guests * Z)

    def from_sibling(role, t):
        for shift in range(Z):
            for part in PARTS[role]:
                if part[0] < 2:
                    sibling(t, shift, part, 1 - c).wait_recv()
            late_sibling(role, t, shift, 1 - c).wait_recv()

    pack_v()
    by_role(lambda role: own_part(role, 0))
    all_rows(1, False)
    by_role(lambda role: pass_on(role, 0, 1, (0, 2)))
    reads[2].wait()
    each_y(lambda i: q_copy(i, False))
    by_role(lambda role: pass_on(role, 0, 1, (1,)))

    def turn(role, t):
        pass_on(role, t + 1, 1)
        pass_on(role, t, 4)
        if role != HELP:
            late_pair(role, t, 3)
            late(role, t, 4)
            from_sibling(role, t)
            late(role, t + 1, 0)

    by_role(lambda role: pass_on(role, 0, 2))
    all_rows(2, False)

    def k_ring(role):
        own_part(role, 1)
        if role != HELP:
            late(role, 0, 0)
            late_pair(role, 0, 1)
        pass_on(role, 0, 3)
        if role != HELP:
            late_pair(role, 0, 2)
        turn(role, 0)

    by_role(k_ring)

    def o_copy(half, n, xq, u, wait):
        src, dst = obuf.at[half, xq, u], oin.at[half, y * HX + x]
        own = (xq == x) & (u == y)

        @pl.when(jnp.logical_not(own))
        def _():
            copy = pltpu.make_async_remote_copy(
                src_ref=src, dst_ref=dst, send_sem=o_send.at[half, n], recv_sem=o_recv.at[half],
                device_id=(blk_at(xq), u), device_id_type=MESH,
            )
            copy.wait_send() if wait else copy.start()

        if not wait:

            @pl.when(own)
            def _():
                pltpu.make_async_copy(src, dst, o_recv.at[half]).start()

    @pl.when(x < HX)
    def _():
        place = jnp.where(x == 1, 16, 8)
        both = (EDGE, MID)

        def cluster(i):
            return (x + 1 + (i >> 1)) & 3, i & 1

        def gather(i, buf):
            xq, s = cluster(i)
            for j in range(SEL):
                at = lists[xq, place + 3 * s, j]
                for n in range(buf.shape[1] // 16):
                    row = n * (KEYS // 2) + j * (LIVE // 2)
                    gath[row : row + LIVE // 2, :] = buf[pl.ds(at, GROUPS), n * 16 : (n + 1) * 16, :].reshape(LIVE // 2, HD)
            return xq, s

        def scores(i, _):
            xq, s = gather(i, kbuf)
            lane = lax.broadcasted_iota(jnp.int32, (1, KEYS), 1)
            low = jnp.where(lane >= KEYS // 2, 1, 0)
            at = lane - low * (KEYS // 2)
            n = at - ((at * 1366) >> 16) * (LIVE // 2)
            row = ((n >> 4) << 5) + (n & 15) + 16 * low
            end = jnp.zeros((1, KEYS), jnp.int32)
            for j in range(SEL):
                end = jnp.where(at >= j * (LIVE // 2), fill_ref[lists[xq, 3 * s, j]], end)
            bias = jnp.where(row < end, 0.0, -1e30)
            for n in range(3):
                rows = pl.ds(pl.multiple_of(s * CROWS + n * TILE, TILE), TILE)
                sc = lax.dot_general(
                    qbuf[xq, rows, :], gath[...], (((1,), (1,)), ((), ())), preferred_element_type=jnp.float32
                )
                sc = sc + bias
                peak = jnp.max(sc, axis=1, keepdims=True)
                w = jnp.exp2((sc - peak) * C2)
                totals[i, n * TILE : (n + 1) * TILE, :] = jnp.sum(w, axis=1, keepdims=True)
                probs[i, n * TILE : (n + 1) * TILE, :] = w.astype(jnp.bfloat16)
            return 0

        def mix(half, i):
            xq, s = gather(i, (vbuf0, vbuf1)[half])
            for w in range(4):
                rows = slice(w * PART, (w + 1) * PART)
                top = jnp.dot(probs[i, rows, : KEYS // 2], gath[: KEYS // 2, :], preferred_element_type=jnp.float32)
                low = jnp.dot(probs[i, rows, KEYS // 2 :], gath[: KEYS // 2, :], preferred_element_type=jnp.float32)
                if half:
                    o = pltpu.roll(top, HD // 2, 1) + low
                else:
                    o = top + pltpu.roll(low, HD // 2, 1)
                o = o / totals[i, rows, :]
                obuf[half, xq, 4 * s + w] = paired(o[: PART // 2], o[PART // 2 :])[half]
            for w in range(4):
                o_copy(half, 4 * i + w, xq, 4 * s + w, False)
            return 0

        def v_step(t, work):
            def step(k, _):
                by_role(lambda role: pass_on(role, t, k, (0, 2)), both)
                lax.fori_loop(4 * k - 8, 4 * k - 6, work, 0)
                by_role(lambda role: pass_on(role, t, k, (1,)), both)
                if t == 1:

                    @pl.when(k == 2)
                    def _():
                        by_role(lambda role: own_part(role, 2), both)

                lax.fori_loop(4 * k - 6, 4 * k - 4, work, 0)
                by_role(lambda role: late_pair(role, t, k - 1), both)
                return 0

            return step

        for j in range(1, X):
            list_arrival(j).wait_recv()
        lrecv[pl.ds(x, 1)] = lsend[...][None]
        copy = pltpu.make_async_copy(lrecv, lists, l_copy.at[0])
        copy.start()
        copy.wait()
        pltpu.make_async_copy(qbuf, qbuf, q_recv.at[0]).wait()

        lax.fori_loop(2, 4, v_step(1, scores), 0)
        by_role(lambda role: turn(role, 1), both)
        lax.fori_loop(2, 4, v_step(2, lambda i, _: mix(0, i)), 0)

        def v_end(role):
            late_pair(role, 2, 3)
            pass_on(role, 2, 4)
            late(role, 2, 4)
            from_sibling(role, 2)

        by_role(v_end, both)
        lax.fori_loop(0, 8, lambda i, _: mix(1, i), 0)

        def done(role):
            for t in (0, 1, 2):
                ring_sent(role, t)

        by_role(done, both)

        def sent(i, _):
            xq, s = cluster(i)
            for half in (0, 1):
                for w in range(4):
                    o_copy(half, 4 * i + w, xq, 4 * s + w, True)
            return 0

        lax.fori_loop(0, 8, sent, 0)

    @pl.when(x == HX)
    def _():
        pass_on(HELP, 1, 2)
        own_part(HELP, 2)
        pass_on(HELP, 1, 3)
        turn(HELP, 1)
        for k in range(2, 5):
            pass_on(HELP, 2, k)
        for j in range(1, X):
            list_arrival(j).wait_recv()
        for t in (0, 1, 2):
            ring_sent(HELP, t)

    for t in (0, 1, 2):
        all_rows(t, True)
    each_y(lambda i: q_copy(i, True))
    for j in range(1, X):
        list_copy(j).wait_send()
    for half in (0, 1):
        pltpu.make_async_copy(oin.at[half], oin.at[half], o_recv.at[half]).wait()
    for h in range(HEADS):
        cols = slice(h * HD, (h + 1) * HD)
        out_ref[0 : PART // 2, cols], out_ref[PART // 2 :, cols] = paired(
            oin[0, h].astype(jnp.float32), oin[1, h].astype(jnp.float32)
        )


def local(queries, keys, values, key_lists, key_fill):
    bf = jnp.bfloat16
    anywhere = pl.BlockSpec(memory_space=pl.ANY)
    dma = pltpu.SemaphoreType.DMA
    return pl.pallas_call(
        kernel,
        out_shape=jax.ShapeDtypeStruct(queries.shape, bf),
        in_specs=[
            anywhere, anywhere, anywhere,
            pl.BlockSpec(memory_space=pltpu.VMEM), pl.BlockSpec(memory_space=pltpu.SMEM),
        ],
        out_specs=pl.BlockSpec(memory_space=pltpu.VMEM),
        scratch_shapes=[
            pltpu.VMEM((PART, HEADS * HD), bf),
            pltpu.VMEM((PART, HEADS * HD), bf),
            pltpu.VMEM((PART, HEADS * HD), bf),
            pltpu.VMEM((HEADS, GROUPS, 32, HD), bf),
            pltpu.VMEM((HEADS, GROUPS, 16, HD), bf),
            pltpu.VMEM((HEADS, GROUPS, 16, HD), bf),
            pltpu.VMEM((Z * C * CHUNK, 32, HD), bf),
            pltpu.VMEM((Z * C * CHUNK, 16, HD), bf),
            pltpu.VMEM((Z * C * CHUNK, 16, HD), bf),
            pltpu.VMEM((X, BLOCK, HD), bf),
            pltpu.VMEM((2, X, Y, PART // 2, HD), bf),
            pltpu.VMEM((2, HEADS, PART // 2, HD), bf),
            pltpu.VMEM((KEYS, HD), bf),
            pltpu.VMEM((2 * X, CROWS, KEYS), bf),
            pltpu.VMEM((2 * X, CROWS, 1), jnp.float32),
            pltpu.VMEM((24, 128), jnp.int32),
            pltpu.VMEM((X, 24, 128), jnp.int32),
            pltpu.SMEM((X, 24, 128), jnp.int32),
            dma((3,)),
            dma((4, HEADS)),
            dma((3, 3)),
            dma((1,)),
            dma((3,)),
            dma((3, 2, 3, 4)),
            dma((3,)),
            dma((3, Z, 2)),
            dma((3,)),
            dma((3, Z, 2)),
            dma((3,)),
            dma((3, Z)),
            dma((X - 1,)),
            dma((X - 1,)),
            dma((1,)),
            dma((2, X * Y)),
            dma((2,)),
        ],
        compiler_params=pltpu.CompilerParams(
            collective_id=0, has_side_effects=True, vmem_limit_bytes=56 * 1024 * 1024
        ),
        cost_estimate=pl.CostEstimate(flops=5_000_000_000, bytes_accessed=4_000_000, transcendentals=4_800_000),
    )(queries, keys, values, key_lists, key_fill)


def solution(mesh):
    in_specs = (
        P(("blk", "uly"), None),
        P(("blk", "uly"), None),
        P(("blk", "uly"), None),
        P("blk", None),
        P(),
    )
    out_specs = P(("blk", "uly"), None)
    return jax.shard_map(local, mesh=mesh, in_specs=in_specs, out_specs=out_specs, check_vma=False)
```

```python
import math

import jax
import jax.numpy as jnp
from jax import lax
from jax.experimental import pallas as pl
from jax.experimental.pallas import tpu as pltpu
from jax.sharding import PartitionSpec as P

HD = 128
TILE = 128
SEL = 16
LIVE = 96
X, Z, C, Y = 4, 8, 2, 8
HX = 3
HEADS = HX * Y
PART = 96
BLOCK = PART * Y
PER = BLOCK // TILE
CROWS = BLOCK // 2
KEYS = SEL * LIVE
GROUPS = LIVE // 32
SLOTS = 26
CHUNK = SLOTS * GROUPS
LATE = 20 * GROUPS
GUEST = 18 * GROUPS
EDGE, MID, HELP = 0, 1, 2
PARTS = {EDGE: ((2, 54, 6), (0, 0, 30), (1, 30, 24)), MID: ((0, 0, 30), (1, 30, 30)), HELP: ((0, 0, 18), (1, 18, 18))}
HOPS = ((4, 3), (3, 4), (3, 4))
MESH = pl.DeviceIdType.MESH
C2 = math.log2(math.e) / math.sqrt(HD)


def kernel(
    q_ref, k_ref, v_ref, list_hbm, fill_hbm, out_ref, list_ref, fill_ref,
    qin, kin, vin, kpack, vpack0, vpack1, kbuf, vbuf0, vbuf1, qbuf, obuf, oin, gath, probs, totals, lsend, lrecv, lists,
    in_sem, p1_send, p1_recv, q_recv, ring_send, ring_recv, sib_send, sib_recv, dl_send, dl_recv, ds_send, ds_recv,
    l_send, l_recv, l_copy, o_send, o_recv,
):
    blk, y = lax.axis_index("blk"), lax.axis_index("uly")
    x, z, c = blk >> 4, (blk >> 1) & 7, blk & 1
    plane = blk & 15
    r, a = y & 3, y >> 2
    role_of = ((x & 1) == 0, x == 1, x == 3)

    def by_role(f, roles=(EDGE, MID, HELP)):
        for role in roles:
            pl.when(role_of[role])(lambda role=role: f(role))

    reads = [
        pltpu.make_async_copy(src, dst, in_sem.at[n])
        for n, (src, dst) in enumerate(((k_ref, kin), (v_ref, vin), (q_ref, qin), (list_hbm, list_ref), (fill_hbm, fill_ref)))
    ]
    for copy in reads:
        copy.start()

    def blk_at(xx):
        return (xx << 4) + plane

    barrier = pltpu.get_barrier_semaphore()
    right = ((blk & 49) + (((z + 1) & 7) << 1), y)
    left = ((blk & 49) + (((z + 7) & 7) << 1), y)
    other = (blk ^ 1, y)
    steps = [(i, j) for j in range(Y) for i in range(X) if i or j]
    steps.sort(key=lambda ij: -min(ij[0], X - ij[0]) - min(ij[1], Y - ij[1]))
    near = [(blk_at((x + i) & 3), (y + j) & 7) for i, j in steps]
    for d in (*near, right, left, other):
        pl.semaphore_signal(barrier, inc=1, device_id=d, device_id_type=MESH)

    piece0 = pl.multiple_of(jnp.where(r == 1, 32, 0), 32)
    piece1 = pl.multiple_of(jnp.where((r == 1) | (r == 2), 64, 32), 32)

    def pieces(src, h):
        cols = slice(h * HD, (h + 1) * HD)
        return src[pl.ds(piece0, 32), cols], src[pl.ds(piece1, 32), cols], src[64:96, cols]

    def pack_k():
        reads[0].wait()
        for h in range(HEADS):
            for g, rows in enumerate(pieces(kin, h)):
                kpack[h, g] = rows

    def paired(top, bottom):
        left = lax.broadcasted_iota(jnp.int32, top.shape, 1) < HD // 2
        return (
            jnp.where(left, top, pltpu.roll(bottom, HD // 2, 1)).astype(jnp.bfloat16),
            jnp.where(left, pltpu.roll(top, HD // 2, 1), bottom).astype(jnp.bfloat16),
        )

    def pack_v():
        reads[1].wait()
        for h in range(HEADS):
            for g, rows in enumerate(pieces(vin, h)):
                rows = rows.astype(jnp.float32)
                vpack0[h, g], vpack1[h, g] = paired(rows[0:16], rows[16:32])

    pack_k()
    pl.semaphore_wait(barrier, len(near) + 3)

    bufs = (kbuf, vbuf0, vbuf1)

    def region(t, zz, core, at, count):
        return bufs[t].at[pl.ds((zz * C + core) * CHUNK + at, count)]

    off = jnp.where(r == 0, 0, 1 + 2 * r)
    wing = (x == 0) | (x == 2)
    i32 = jnp.int32

    def target(xh):
        if xh != 1:
            helped = x == 3
            xd = jnp.where(helped, 3, xh)
            at = jnp.where(helped, (PER if xh else 0), x * PER) * GROUPS + 9 * a + off
            half = jnp.where(helped, xh // 2, jnp.where((x == 2) | ((x == 1) & (a == 1) & (r != 0)), 1, 0))
            return xd, at, half
        guest = wing & (r == 0)
        xd = jnp.where(guest, x, 1)
        own = jnp.where(wing, 5 * x * GROUPS + 6 * a + off - 3, jnp.where(x == 1, 4, 14) * GROUPS + 9 * a + off)
        at = jnp.where(guest, GUEST + GROUPS * a, own)
        half = jnp.where(guest, 2, jnp.where(x >= 2, 1, 0))
        return xd, at, half

    targets = [target(xh) for xh in range(HX)]

    def far_first(i):
        return (y + jnp.where(i & 1 == 1, 4 - ((i + 1) >> 1), 4 + (i >> 1))) & 7

    def rows_copy(t, i, rows, wait):
        yh = far_first(i)
        for xh, (xd, at, half) in enumerate(targets):
            own = (xd == x) & (yh == y)
            src = (kpack, vpack0, vpack1)[t].at[yh * HX + xh, pl.ds(0, rows)]
            dst = region(t, z, c, at, rows)

            @pl.when(jnp.logical_not(own))
            def _():
                copy = pltpu.make_async_remote_copy(
                    src_ref=src, dst_ref=dst, send_sem=p1_send.at[t, i * HX + xh], recv_sem=p1_recv.at[t, half],
                    device_id=(blk_at(xd), yh), device_id_type=MESH,
                )
                copy.wait_send() if wait else copy.start()

            if not wait:

                @pl.when(own)
                def _():
                    pltpu.make_async_copy(src, dst, p1_recv.at[t, half]).start()

    def q_copy(i, wait):
        yh = far_first(i)
        for xh in range(HX):
            own = (xh == x) & (yh == y)
            src = qin.at[:, pl.ds(pl.multiple_of((yh * HX + xh) * HD, HD), HD)]
            dst = qbuf.at[x, pl.ds(pl.multiple_of(y * PART, 32), PART)]

            @pl.when(jnp.logical_not(own))
            def _():
                copy = pltpu.make_async_remote_copy(
                    src_ref=src, dst_ref=dst, send_sem=p1_send.at[3, i * HX + xh], recv_sem=q_recv.at[0],
                    device_id=(blk_at(xh), yh), device_id_type=MESH,
                )
                copy.wait_send() if wait else copy.start()

            if not wait:

                @pl.when(own)
                def _():
                    pltpu.make_async_copy(src, dst, q_recv.at[0]).start()

    def each_y(body):
        def step(i, _):
            body(i)
            return 0

        lax.fori_loop(0, Y, step, 0)

    def all_rows(t, wait):
        @pl.when(r == 0)
        def _():
            each_y(lambda i: rows_copy(t, i, 3, wait))

        @pl.when(r != 0)
        def _():
            each_y(lambda i: rows_copy(t, i, 2, wait))

    all_rows(0, False)

    reads[3].wait()
    reads[4].wait()
    lsend[...] = jnp.zeros_like(lsend)
    tile = list_ref[...]
    owner = (tile * 10923) >> 16
    n = tile - owner * PER
    ox = owner >> 4
    start = (owner & (Z * C - 1)) * SLOTS
    edge = ox * PER + n + jnp.where(ox == 3, 2, 0)
    first = (n == 0) | (n == 3)
    outer = jnp.where(first, 20 + ox + jnp.where(n == 3, 1, 0), ox * 5 + n - 1 - jnp.where(n > 3, 1, 0))
    inner = jnp.where(ox == 1, 4, 14) + n
    middle = jnp.where((ox == 0) | (ox == 2), outer, inner)
    lsend[0:PER, 0:SEL] = tile
    lsend[8 : 8 + PER, 0:SEL] = (start + edge) * GROUPS
    lsend[16 : 16 + PER, 0:SEL] = (start + middle) * GROUPS

    def list_copy(j):
        return pltpu.make_async_remote_copy(
            src_ref=lsend, dst_ref=lrecv.at[x], send_sem=l_send.at[j - 1], recv_sem=l_recv.at[j - 1],
            device_id=(blk_at((x + j) % X), y), device_id_type=MESH,
        )

    def list_arrival(j):
        return pltpu.make_async_remote_copy(
            src_ref=lsend, dst_ref=lrecv.at[(x + X - j) % X], send_sem=l_send.at[j - 1], recv_sem=l_recv.at[j - 1],
            device_id=(blk_at((x + j) % X), y), device_id_type=MESH,
        )

    for j in range(1, X):
        list_copy(j).start()

    def ring_copy(t, way, part, k, distance):
        n, at, size = part
        origin = (z + (Z - distance if way == 0 else distance)) & 7
        rows = region(t, origin, c, at, size)
        return pltpu.make_async_remote_copy(
            src_ref=rows, dst_ref=rows, send_sem=ring_send.at[t], recv_sem=ring_recv.at[t, way, n, k - 1],
            device_id=(right, left)[way], device_id_type=MESH,
        )

    def sibling(t, shift, part, core):
        n, at, size = part
        rows = region(t, (z + shift) & 7, core, at, size)
        return pltpu.make_async_remote_copy(
            src_ref=rows, dst_ref=rows, send_sem=sib_send.at[t], recv_sem=sib_recv.at[t, shift, n],
            device_id=other, device_id_type=MESH,
        )

    def guest(t, shift):
        origin = (z + shift) & 7
        return pltpu.make_async_remote_copy(
            src_ref=region(t, origin, c, GUEST, 2 * GROUPS), dst_ref=region(t, origin, c, LATE + GROUPS * x, 2 * GROUPS),
            send_sem=dl_send.at[t], recv_sem=dl_recv.at[t, shift, x >> 1],
            device_id=(blk_at(1), y), device_id_type=MESH,
        )

    def hand_over(t, shift, part):
        n, at, size = part
        origin = (z + shift) & 7
        return pltpu.make_async_remote_copy(
            src_ref=region(t, origin, c, at, size), dst_ref=region(t, origin, c, LATE, size),
            send_sem=dl_send.at[t], recv_sem=dl_recv.at[t, shift, 0],
            device_id=(blk_at(2 * n), y), device_id_type=MESH,
        )

    def late_sibling(role, t, shift, core):
        rows = region(t, (z + shift) & 7, core, LATE, (18, 12)[role])
        return pltpu.make_async_remote_copy(
            src_ref=rows, dst_ref=rows, send_sem=ds_send.at[t], recv_sem=ds_recv.at[t, shift],
            device_id=other, device_id_type=MESH,
        )

    def spread(role, t, shift, part):
        if role == HELP:
            hand_over(t, shift, part).start()
        elif part[0] == 2:
            guest(t, shift).start()
        else:
            sibling(t, shift, part, c).start()

    def late(role, t, shift):
        size = (18, 6)[role]
        for n in range((1, 2)[role]):
            rows = region(t, (z + shift) & 7, c, LATE + size * n, size)
            pltpu.make_async_copy(rows, rows, dl_recv.at[t, shift, n]).wait()
        late_sibling(role, t, shift, c).start()

    def late_pair(role, t, k):
        late(role, t, k)
        late(role, t, Z - k)

    def own_part(role, t):
        for part in PARTS[role]:
            n, at, size = part
            rows = region(t, z, c, at, size)
            pltpu.make_async_copy(rows, rows, p1_recv.at[t, n]).wait()
            for way in (0, 1):
                ring_copy(t, way, part, 1, 0).start()
            spread(role, t, 0, part)

    def pass_on(role, t, k, parts=(0, 1, 2)):
        for part in PARTS[role]:
            n = part[0]
            if n not in parts:
                continue
            for way in (0, 1):
                last = HOPS[n][way]
                if isinstance(k, int) and k > last:
                    continue
                ring_copy(t, way, part, k, k).wait_recv()
                if isinstance(k, int):
                    if k < last:
                        ring_copy(t, way, part, k + 1, k).start()
                elif last == 4:
                    ring_copy(t, way, part, k + 1, k).start()
                else:

                    @pl.when(k < last)
                    def _():
                        ring_copy(t, way, part, k + 1, k).start()

                spread(role, t, (Z - k) if way == 0 else k, part)

    def sent_all(t, sem, groups):
        rows = bufs[t].at[pl.ds(0, groups)]
        pltpu.make_async_copy(rows, rows, sem.at[t]).wait()

    def ring_sent(role, t):
        sizes = [size for n, _, size in PARTS[role] if n < 2]
        guests = 6 if role == EDGE else 0
        sent_all(t, ring_send, (sum(sizes) + guests) * (Z - 1))
        if role == HELP:
            sent_all(t, dl_send, sum(sizes) * Z)
            return
        sent_all(t, sib_send, sum(sizes) * Z)
        sent_all(t, ds_send, (18, 12)[role] * Z)
        if guests:
            sent_all(t, dl_send, guests * Z)

    def from_sibling(role, t):
        for shift in range(Z):
            for part in PARTS[role]:
                if part[0] < 2:
                    sibling(t, shift, part, 1 - c).wait_recv()
            late_sibling(role, t, shift, 1 - c).wait_recv()

    pack_v()
    by_role(lambda role: own_part(role, 0))
    all_rows(1, False)
    by_role(lambda role: pass_on(role, 0, 1, (0, 2)))
    reads[2].wait()
    each_y(lambda i: q_copy(i, False))
    by_role(lambda role: pass_on(role, 0, 1, (1,)))

    def turn(role, t):
        pass_on(role, t + 1, 1)
        pass_on(role, t, 4)
        if role != HELP:
            late_pair(role, t, 3)
            late(role, t, 4)
            from_sibling(role, t)
            late(role, t + 1, 0)

    by_role(lambda role: pass_on(role, 0, 2))
    all_rows(2, False)

    def k_ring(role):
        own_part(role, 1)
        if role != HELP:
            late(role, 0, 0)
            late_pair(role, 0, 1)
        pass_on(role, 0, 3)
        if role != HELP:
            late_pair(role, 0, 2)
        turn(role, 0)

    by_role(k_ring)

    def o_copy(half, n, xq, u, wait):
        src, dst = obuf.at[half, xq, u], oin.at[half, y * HX + x]
        own = (xq == x) & (u == y)

        @pl.when(jnp.logical_not(own))
        def _():
            copy = pltpu.make_async_remote_copy(
                src_ref=src, dst_ref=dst, send_sem=o_send.at[half, n], recv_sem=o_recv.at[half],
                device_id=(blk_at(xq), u), device_id_type=MESH,
            )
            copy.wait_send() if wait else copy.start()

        if not wait:

            @pl.when(own)
            def _():
                pltpu.make_async_copy(src, dst, o_recv.at[half]).start()

    @pl.when(x < HX)
    def _():
        place = jnp.where(x == 1, 16, 8)
        both = (EDGE, MID)

        def cluster(i):
            return (x + 1 + (i >> 1)) & 3, i & 1

        def gather(i, buf):
            xq, s = cluster(i)
            for j in range(SEL):
                at = lists[xq, place + 3 * s, j]
                for n in range(buf.shape[1] // 16):
                    row = n * (KEYS // 2) + j * (LIVE // 2)
                    gath[row : row + LIVE // 2, :] = buf[pl.ds(at, GROUPS), n * 16 : (n + 1) * 16, :].reshape(LIVE // 2, HD)
            return xq, s

        def scores(i, _):
            xq, s = gather(i, kbuf)
            lane = lax.broadcasted_iota(jnp.int32, (1, KEYS), 1)
            low = jnp.where(lane >= KEYS // 2, 1, 0)
            at = lane - low * (KEYS // 2)
            n = at - ((at * 1366) >> 16) * (LIVE // 2)
            row = ((n >> 4) << 5) + (n & 15) + 16 * low
            end = jnp.zeros((1, KEYS), jnp.int32)
            for j in range(SEL):
                end = jnp.where(at >= j * (LIVE // 2), fill_ref[lists[xq, 3 * s, j]], end)
            bias = jnp.where(row < end, 0.0, -1e30)
            for n in range(3):
                rows = pl.ds(pl.multiple_of(s * CROWS + n * TILE, TILE), TILE)
                sc = lax.dot_general(
                    qbuf[xq, rows, :], gath[...], (((1,), (1,)), ((), ())), preferred_element_type=jnp.float32
                )
                sc = sc + bias
                peak = jnp.max(sc, axis=1, keepdims=True)
                w = jnp.exp2((sc - peak) * C2)
                totals[i, n * TILE : (n + 1) * TILE, :] = jnp.sum(w, axis=1, keepdims=True)
                probs[i, n * TILE : (n + 1) * TILE, :] = w.astype(jnp.bfloat16)
            return 0

        def mix(half, i):
            xq, s = gather(i, (vbuf0, vbuf1)[half])
            for w in range(4):
                rows = slice(w * PART, (w + 1) * PART)
                top = jnp.dot(probs[i, rows, : KEYS // 2], gath[: KEYS // 2, :], preferred_element_type=jnp.float32)
                low = jnp.dot(probs[i, rows, KEYS // 2 :], gath[: KEYS // 2, :], preferred_element_type=jnp.float32)
                if half:
                    o = pltpu.roll(top, HD // 2, 1) + low
                else:
                    o = top + pltpu.roll(low, HD // 2, 1)
                o = o / totals[i, rows, :]
                obuf[half, xq, 4 * s + w] = paired(o[: PART // 2], o[PART // 2 :])[half]
            for w in range(4):
                o_copy(half, 4 * i + w, xq, 4 * s + w, False)
            return 0

        def v_step(t, work):
            def step(k, _):
                by_role(lambda role: pass_on(role, t, k, (0, 2)), both)
                lax.fori_loop(4 * k - 8, 4 * k - 6, work, 0)
                by_role(lambda role: pass_on(role, t, k, (1,)), both)
                if t == 1:

                    @pl.when(k == 2)
                    def _():
                        by_role(lambda role: own_part(role, 2), both)

                lax.fori_loop(4 * k - 6, 4 * k - 4, work, 0)
                by_role(lambda role: late_pair(role, t, k - 1), both)
                return 0

            return step

        for j in range(1, X):
            list_arrival(j).wait_recv()
        lrecv[pl.ds(x, 1)] = lsend[...][None]
        copy = pltpu.make_async_copy(lrecv, lists, l_copy.at[0])
        copy.start()
        copy.wait()
        pltpu.make_async_copy(qbuf, qbuf, q_recv.at[0]).wait()

        lax.fori_loop(2, 4, v_step(1, scores), 0)
        by_role(lambda role: turn(role, 1), both)
        lax.fori_loop(2, 4, v_step(2, lambda i, _: mix(0, i)), 0)

        def v_end(role):
            late_pair(role, 2, 3)
            pass_on(role, 2, 4)
            late(role, 2, 4)
            from_sibling(role, 2)

        by_role(v_end, both)
        lax.fori_loop(0, 8, lambda i, _: mix(1, i), 0)

        def done(role):
            for t in (0, 1, 2):
                ring_sent(role, t)

        by_role(done, both)

        def sent(i, _):
            xq, s = cluster(i)
            for half in (0, 1):
                for w in range(4):
                    o_copy(half, 4 * i + w, xq, 4 * s + w, True)
            return 0

        lax.fori_loop(0, 8, sent, 0)

    @pl.when(x == HX)
    def _():
        pass_on(HELP, 1, 2)
        own_part(HELP, 2)
        pass_on(HELP, 1, 3)
        turn(HELP, 1)
        for k in range(2, 5):
            pass_on(HELP, 2, k)
        for j in range(1, X):
            list_arrival(j).wait_recv()
        for t in (0, 1, 2):
            ring_sent(HELP, t)

    for t in (0, 1, 2):
        all_rows(t, True)
    each_y(lambda i: q_copy(i, True))
    for j in range(1, X):
        list_copy(j).wait_send()
    for half in (0, 1):
        pltpu.make_async_copy(oin.at[half], oin.at[half], o_recv.at[half]).wait()
    for h in range(HEADS):
        cols = slice(h * HD, (h + 1) * HD)
        out_ref[0 : PART // 2, cols], out_ref[PART // 2 :, cols] = paired(
            oin[0, h].astype(jnp.float32), oin[1, h].astype(jnp.float32)
        )


def local(queries, keys, values, key_lists, key_fill):
    bf = jnp.bfloat16
    anywhere = pl.BlockSpec(memory_space=pl.ANY)
    dma = pltpu.SemaphoreType.DMA
    return pl.pallas_call(
        kernel,
        out_shape=jax.ShapeDtypeStruct(queries.shape, bf),
        in_specs=[
            anywhere, anywhere, anywhere,
            anywhere, anywhere,
        ],
        out_specs=pl.BlockSpec(memory_space=pltpu.VMEM),
        scratch_shapes=[
            pltpu.VMEM((PER, SEL), jnp.int32),
            pltpu.SMEM((X * Z * C * PER,), jnp.int32),
            pltpu.VMEM((PART, HEADS * HD), bf),
            pltpu.VMEM((PART, HEADS * HD), bf),
            pltpu.VMEM((PART, HEADS * HD), bf),
            pltpu.VMEM((HEADS, GROUPS, 32, HD), bf),
            pltpu.VMEM((HEADS, GROUPS, 16, HD), bf),
            pltpu.VMEM((HEADS, GROUPS, 16, HD), bf),
            pltpu.VMEM((Z * C * CHUNK, 32, HD), bf),
            pltpu.VMEM((Z * C * CHUNK, 16, HD), bf),
            pltpu.VMEM((Z * C * CHUNK, 16, HD), bf),
            pltpu.VMEM((X, BLOCK, HD), bf),
            pltpu.VMEM((2, X, Y, PART // 2, HD), bf),
            pltpu.VMEM((2, HEADS, PART // 2, HD), bf),
            pltpu.VMEM((KEYS, HD), bf),
            pltpu.VMEM((2 * X, CROWS, KEYS), bf),
            pltpu.VMEM((2 * X, CROWS, 1), jnp.float32),
            pltpu.VMEM((24, 128), jnp.int32),
            pltpu.VMEM((X, 24, 128), jnp.int32),
            pltpu.SMEM((X, 24, 128), jnp.int32),
            dma((5,)),
            dma((4, HEADS)),
            dma((3, 3)),
            dma((1,)),
            dma((3,)),
            dma((3, 2, 3, 4)),
            dma((3,)),
            dma((3, Z, 2)),
            dma((3,)),
            dma((3, Z, 2)),
            dma((3,)),
            dma((3, Z)),
            dma((X - 1,)),
            dma((X - 1,)),
            dma((1,)),
            dma((2, X * Y)),
            dma((2,)),
        ],
        compiler_params=pltpu.CompilerParams(
            collective_id=0, has_side_effects=True, vmem_limit_bytes=56 * 1024 * 1024
        ),
        cost_estimate=pl.CostEstimate(flops=5_000_000_000, bytes_accessed=4_000_000, transcendentals=4_800_000),
    )(queries, keys, values, key_lists, key_fill)


def solution(mesh):
    in_specs = (
        P(("blk", "uly"), None),
        P(("blk", "uly"), None),
        P(("blk", "uly"), None),
        P("blk", None),
        P(),
    )
    out_specs = P(("blk", "uly"), None)
    return jax.shard_map(local, mesh=mesh, in_specs=in_specs, out_specs=out_specs, check_vma=False)
```

```python
import math

import jax
import jax.numpy as jnp
from jax import lax
from jax.experimental import pallas as pl
from jax.experimental.pallas import tpu as pltpu
from jax.sharding import PartitionSpec as P

HD = 128
TILE = 128
SEL = 16
LIVE = 96
X, Z, C, Y = 4, 8, 2, 8
HX = 3
HEADS = HX * Y
PART = 96
BLOCK = PART * Y
PER = BLOCK // TILE
CROWS = BLOCK // 2
KEYS = SEL * LIVE
GROUPS = LIVE // 32
SLOTS = 26
CHUNK = SLOTS * GROUPS
LATE = 20 * GROUPS
GUEST = 18 * GROUPS
EDGE, MID, HELP = 0, 1, 2
PARTS = {EDGE: ((2, 54, 6), (0, 0, 30), (1, 30, 24)), MID: ((0, 0, 30), (1, 30, 30)), HELP: ((0, 0, 18), (1, 18, 18))}
HOPS = ((4, 3), (3, 4), (3, 4))
MESH = pl.DeviceIdType.MESH
C2 = math.log2(math.e) / math.sqrt(HD)


def kernel(
    q_ref, k_ref, v_ref, list_hbm, fill_hbm, out_ref, list_ref, fill_ref,
    qin, kin, vin, kpack, vpack0, vpack1, kbuf, vbuf0, vbuf1, qbuf, obuf, oin, gath, probs, totals, lsend, lrecv, lists,
    in_sem, p1_send, p1_recv, q_recv, ring_send, ring_recv, sib_send, sib_recv, dl_send, dl_recv, ds_send, ds_recv,
    l_send, l_recv, l_copy, o_send, o_recv,
):
    blk, y = lax.axis_index("blk"), lax.axis_index("uly")
    x, z, c = blk >> 4, (blk >> 1) & 7, blk & 1
    plane = blk & 15
    r, a = y & 3, y >> 2
    role_of = ((x & 1) == 0, x == 1, x == 3)

    def by_role(f, roles=(EDGE, MID, HELP)):
        for role in roles:
            pl.when(role_of[role])(lambda role=role: f(role))

    reads = [
        pltpu.make_async_copy(src, dst, in_sem.at[n])
        for n, (src, dst) in enumerate(((k_ref, kin), (v_ref, vin), (q_ref, qin), (list_hbm, list_ref), (fill_hbm, fill_ref)))
    ]
    for copy in reads:
        copy.start()

    def blk_at(xx):
        return (xx << 4) + plane

    barrier = pltpu.get_barrier_semaphore()
    right = ((blk & 49) + (((z + 1) & 7) << 1), y)
    left = ((blk & 49) + (((z + 7) & 7) << 1), y)
    other = (blk ^ 1, y)
    steps = [(i, j) for j in range(Y) for i in range(X) if i or j]
    steps.sort(key=lambda ij: -min(ij[0], X - ij[0]) - min(ij[1], Y - ij[1]))
    near = [(blk_at((x + i) & 3), (y + j) & 7) for i, j in steps]
    for d in (*near, right, left, other):
        pl.semaphore_signal(barrier, inc=1, device_id=d, device_id_type=MESH)

    piece0 = pl.multiple_of(jnp.where(r == 1, 32, 0), 32)
    piece1 = pl.multiple_of(jnp.where((r == 1) | (r == 2), 64, 32), 32)

    def pieces(src, h):
        cols = slice(h * HD, (h + 1) * HD)
        return src[pl.ds(piece0, 32), cols], src[pl.ds(piece1, 32), cols], src[64:96, cols]

    def pack_k():
        reads[0].wait()
        for h in range(HEADS):
            for g, rows in enumerate(pieces(kin, h)):
                kpack[h, g] = rows

    def paired(top, bottom):
        left = lax.broadcasted_iota(jnp.int32, top.shape, 1) < HD // 2
        return (
            jnp.where(left, top, pltpu.roll(bottom, HD // 2, 1)).astype(jnp.bfloat16),
            jnp.where(left, pltpu.roll(top, HD // 2, 1), bottom).astype(jnp.bfloat16),
        )

    def pack_v():
        reads[1].wait()
        for h in range(HEADS):
            for g, rows in enumerate(pieces(vin, h)):
                rows = rows.astype(jnp.float32)
                vpack0[h, g], vpack1[h, g] = paired(rows[0:16], rows[16:32])

    pack_k()
    pl.semaphore_wait(barrier, len(near) + 3)

    bufs = (kbuf, vbuf0, vbuf1)

    def region(t, zz, core, at, count):
        return bufs[t].at[pl.ds((zz * C + core) * CHUNK + at, count)]

    off = jnp.where(r == 0, 0, 1 + 2 * r)
    wing = (x == 0) | (x == 2)
    i32 = jnp.int32

    def target(xh):
        if xh != 1:
            helped = x == 3
            xd = jnp.where(helped, 3, xh)
            at = jnp.where(helped, (PER if xh else 0), x * PER) * GROUPS + 9 * a + off
            half = jnp.where(helped, xh // 2, jnp.where((x == 2) | ((x == 1) & (a == 1) & (r != 0)), 1, 0))
            return xd, at, half
        guest = wing & (r == 0)
        xd = jnp.where(guest, x, 1)
        own = jnp.where(wing, 5 * x * GROUPS + 6 * a + off - 3, jnp.where(x == 1, 4, 14) * GROUPS + 9 * a + off)
        at = jnp.where(guest, GUEST + GROUPS * a, own)
        half = jnp.where(guest, 2, jnp.where(x >= 2, 1, 0))
        return xd, at, half

    targets = [target(xh) for xh in range(HX)]

    def far_first(i):
        return (y + jnp.where(i & 1 == 1, 4 - ((i + 1) >> 1), 4 + (i >> 1))) & 7

    def rows_copy(t, i, rows, wait):
        yh = far_first(i)
        for xh, (xd, at, half) in enumerate(targets):
            own = (xd == x) & (yh == y)
            src = (kpack, vpack0, vpack1)[t].at[yh * HX + xh, pl.ds(0, rows)]
            dst = region(t, z, c, at, rows)

            @pl.when(jnp.logical_not(own))
            def _():
                copy = pltpu.make_async_remote_copy(
                    src_ref=src, dst_ref=dst, send_sem=p1_send.at[t, i * HX + xh], recv_sem=p1_recv.at[t, half],
                    device_id=(blk_at(xd), yh), device_id_type=MESH,
                )
                copy.wait_send() if wait else copy.start()

            if not wait:

                @pl.when(own)
                def _():
                    pltpu.make_async_copy(src, dst, p1_recv.at[t, half]).start()

    def q_copy(i, wait):
        yh = far_first(i)
        for xh in range(HX):
            own = (xh == x) & (yh == y)
            src = qin.at[:, pl.ds(pl.multiple_of((yh * HX + xh) * HD, HD), HD)]
            dst = qbuf.at[x, pl.ds(pl.multiple_of(y * PART, 32), PART)]

            @pl.when(jnp.logical_not(own))
            def _():
                copy = pltpu.make_async_remote_copy(
                    src_ref=src, dst_ref=dst, send_sem=p1_send.at[3, i * HX + xh], recv_sem=q_recv.at[0],
                    device_id=(blk_at(xh), yh), device_id_type=MESH,
                )
                copy.wait_send() if wait else copy.start()

            if not wait:

                @pl.when(own)
                def _():
                    pltpu.make_async_copy(src, dst, q_recv.at[0]).start()

    def each_y(body):
        def step(i, _):
            body(i)
            return 0

        lax.fori_loop(0, Y, step, 0)

    def all_rows(t, wait):
        @pl.when(r == 0)
        def _():
            each_y(lambda i: rows_copy(t, i, 3, wait))

        @pl.when(r != 0)
        def _():
            each_y(lambda i: rows_copy(t, i, 2, wait))

    all_rows(0, False)

    reads[3].wait()
    reads[4].wait()
    lsend[...] = jnp.zeros_like(lsend)
    tile = list_ref[...]
    owner = (tile * 10923) >> 16
    n = tile - owner * PER
    ox = owner >> 4
    start = (owner & (Z * C - 1)) * SLOTS
    edge = ox * PER + n + jnp.where(ox == 3, 2, 0)
    first = (n == 0) | (n == 3)
    outer = jnp.where(first, 20 + ox + jnp.where(n == 3, 1, 0), ox * 5 + n - 1 - jnp.where(n > 3, 1, 0))
    inner = jnp.where(ox == 1, 4, 14) + n
    middle = jnp.where((ox == 0) | (ox == 2), outer, inner)
    lsend[0:PER, 0:SEL] = tile
    lsend[8 : 8 + PER, 0:SEL] = (start + edge) * GROUPS
    lsend[16 : 16 + PER, 0:SEL] = (start + middle) * GROUPS

    def list_copy(j):
        return pltpu.make_async_remote_copy(
            src_ref=lsend, dst_ref=lrecv.at[x], send_sem=l_send.at[j - 1], recv_sem=l_recv.at[j - 1],
            device_id=(blk_at((x + j) % X), y), device_id_type=MESH,
        )

    def list_arrival(j):
        return pltpu.make_async_remote_copy(
            src_ref=lsend, dst_ref=lrecv.at[(x + X - j) % X], send_sem=l_send.at[j - 1], recv_sem=l_recv.at[j - 1],
            device_id=(blk_at((x + j) % X), y), device_id_type=MESH,
        )

    for j in range(1, X):
        list_copy(j).start()

    def ring_copy(t, way, part, k, distance):
        n, at, size = part
        origin = (z + (Z - distance if way == 0 else distance)) & 7
        rows = region(t, origin, c, at, size)
        return pltpu.make_async_remote_copy(
            src_ref=rows, dst_ref=rows, send_sem=ring_send.at[t], recv_sem=ring_recv.at[t, way, n, k - 1],
            device_id=(right, left)[way], device_id_type=MESH,
        )

    def sibling(t, shift, part, core):
        n, at, size = part
        rows = region(t, (z + shift) & 7, core, at, size)
        return pltpu.make_async_remote_copy(
            src_ref=rows, dst_ref=rows, send_sem=sib_send.at[t], recv_sem=sib_recv.at[t, shift, n],
            device_id=other, device_id_type=MESH,
        )

    def guest(t, shift):
        origin = (z + shift) & 7
        return pltpu.make_async_remote_copy(
            src_ref=region(t, origin, c, GUEST, 2 * GROUPS), dst_ref=region(t, origin, c, LATE + GROUPS * x, 2 * GROUPS),
            send_sem=dl_send.at[t], recv_sem=dl_recv.at[t, shift, x >> 1],
            device_id=(blk_at(1), y), device_id_type=MESH,
        )

    def hand_over(t, shift, part):
        n, at, size = part
        origin = (z + shift) & 7
        return pltpu.make_async_remote_copy(
            src_ref=region(t, origin, c, at, size), dst_ref=region(t, origin, c, LATE, size),
            send_sem=dl_send.at[t], recv_sem=dl_recv.at[t, shift, 0],
            device_id=(blk_at(2 * n), y), device_id_type=MESH,
        )

    def late_sibling(role, t, shift, core):
        rows = region(t, (z + shift) & 7, core, LATE, (18, 12)[role])
        return pltpu.make_async_remote_copy(
            src_ref=rows, dst_ref=rows, send_sem=ds_send.at[t], recv_sem=ds_recv.at[t, shift],
            device_id=other, device_id_type=MESH,
        )

    def spread(role, t, shift, part):
        if role == HELP:
            hand_over(t, shift, part).start()
        elif part[0] == 2:
            guest(t, shift).start()
        else:
            sibling(t, shift, part, c).start()

    def late(role, t, shift):
        size = (18, 6)[role]
        for n in range((1, 2)[role]):
            rows = region(t, (z + shift) & 7, c, LATE + size * n, size)
            pltpu.make_async_copy(rows, rows, dl_recv.at[t, shift, n]).wait()
        late_sibling(role, t, shift, c).start()

    def late_pair(role, t, k):
        late(role, t, k)
        late(role, t, Z - k)

    def own_part(role, t):
        for part in PARTS[role]:
            n, at, size = part
            rows = region(t, z, c, at, size)
            pltpu.make_async_copy(rows, rows, p1_recv.at[t, n]).wait()
            for way in (0, 1):
                ring_copy(t, way, part, 1, 0).start()
            spread(role, t, 0, part)

    def pass_on(role, t, k, parts=(0, 1, 2)):
        for part in PARTS[role]:
            n = part[0]
            if n not in parts:
                continue
            for way in (0, 1):
                last = HOPS[n][way]
                if isinstance(k, int) and k > last:
                    continue
                ring_copy(t, way, part, k, k).wait_recv()
                if isinstance(k, int):
                    if k < last:
                        ring_copy(t, way, part, k + 1, k).start()
                elif last == 4:
                    ring_copy(t, way, part, k + 1, k).start()
                else:

                    @pl.when(k < last)
                    def _():
                        ring_copy(t, way, part, k + 1, k).start()

                spread(role, t, (Z - k) if way == 0 else k, part)

    def sent_all(t, sem, groups):
        rows = bufs[t].at[pl.ds(0, groups)]
        pltpu.make_async_copy(rows, rows, sem.at[t]).wait()

    def ring_sent(role, t):
        sizes = [size for n, _, size in PARTS[role] if n < 2]
        guests = 6 if role == EDGE else 0
        sent_all(t, ring_send, (sum(sizes) + guests) * (Z - 1))
        if role == HELP:
            sent_all(t, dl_send, sum(sizes) * Z)
            return
        sent_all(t, sib_send, sum(sizes) * Z)
        sent_all(t, ds_send, (18, 12)[role] * Z)
        if guests:
            sent_all(t, dl_send, guests * Z)

    def from_sibling(role, t):
        for shift in range(Z):
            for part in PARTS[role]:
                if part[0] < 2:
                    sibling(t, shift, part, 1 - c).wait_recv()
            late_sibling(role, t, shift, 1 - c).wait_recv()

    pack_v()
    by_role(lambda role: own_part(role, 0))
    all_rows(1, False)
    by_role(lambda role: pass_on(role, 0, 1, (0, 2)))
    reads[2].wait()
    each_y(lambda i: q_copy(i, False))
    by_role(lambda role: pass_on(role, 0, 1, (1,)))

    def turn(role, t):
        pass_on(role, t + 1, 1)
        pass_on(role, t, 4)
        if role != HELP:
            late_pair(role, t, 3)
            late(role, t, 4)
            from_sibling(role, t)
            late(role, t + 1, 0)

    by_role(lambda role: pass_on(role, 0, 2))
    all_rows(2, False)

    def k_ring(role):
        own_part(role, 1)
        if role != HELP:
            late(role, 0, 0)
            late_pair(role, 0, 1)
        pass_on(role, 0, 3)
        if role != HELP:
            late_pair(role, 0, 2)
        turn(role, 0)

    by_role(k_ring)

    def o_copy(half, n, xq, u, wait):
        src, dst = obuf.at[half, xq, u], oin.at[half, y * HX + x]
        own = (xq == x) & (u == y)

        @pl.when(jnp.logical_not(own))
        def _():
            copy = pltpu.make_async_remote_copy(
                src_ref=src, dst_ref=dst, send_sem=o_send.at[half, n], recv_sem=o_recv.at[half],
                device_id=(blk_at(xq), u), device_id_type=MESH,
            )
            copy.wait_send() if wait else copy.start()

        if not wait:

            @pl.when(own)
            def _():
                pltpu.make_async_copy(src, dst, o_recv.at[half]).start()

    @pl.when(x < HX)
    def _():
        place = jnp.where(x == 1, 16, 8)
        both = (EDGE, MID)

        def cluster(i):
            return (x + 1 + (i >> 1)) & 3, (i & 1) ^ (1 - a)

        def gather(i, buf):
            xq, s = cluster(i)
            for j in range(SEL):
                at = lists[xq, place + 3 * s, j]
                for n in range(buf.shape[1] // 16):
                    row = n * (KEYS // 2) + j * (LIVE // 2)
                    gath[row : row + LIVE // 2, :] = buf[pl.ds(at, GROUPS), n * 16 : (n + 1) * 16, :].reshape(LIVE // 2, HD)
            return xq, s

        def scores(i, _):
            xq, s = gather(i, kbuf)
            lane = lax.broadcasted_iota(jnp.int32, (1, KEYS), 1)
            low = jnp.where(lane >= KEYS // 2, 1, 0)
            at = lane - low * (KEYS // 2)
            n = at - ((at * 1366) >> 16) * (LIVE // 2)
            row = ((n >> 4) << 5) + (n & 15) + 16 * low
            end = jnp.zeros((1, KEYS), jnp.int32)
            for j in range(SEL):
                end = jnp.where(at >= j * (LIVE // 2), fill_ref[lists[xq, 3 * s, j]], end)
            bias = jnp.where(row < end, 0.0, -1e30)
            for n in range(3):
                rows = pl.ds(pl.multiple_of(s * CROWS + n * TILE, TILE), TILE)
                sc = lax.dot_general(
                    qbuf[xq, rows, :], gath[...], (((1,), (1,)), ((), ())), preferred_element_type=jnp.float32
                )
                sc = sc + bias
                peak = jnp.max(sc, axis=1, keepdims=True)
                w = jnp.exp2((sc - peak) * C2)
                totals[i, n * TILE : (n + 1) * TILE, :] = jnp.sum(w, axis=1, keepdims=True)
                probs[i, n * TILE : (n + 1) * TILE, :] = w.astype(jnp.bfloat16)
            return 0

        def mix(half, i):
            xq, s = gather(i, (vbuf0, vbuf1)[half])
            for w in range(4):
                rows = slice(w * PART, (w + 1) * PART)
                top = jnp.dot(probs[i, rows, : KEYS // 2], gath[: KEYS // 2, :], preferred_element_type=jnp.float32)
                low = jnp.dot(probs[i, rows, KEYS // 2 :], gath[: KEYS // 2, :], preferred_element_type=jnp.float32)
                if half:
                    o = pltpu.roll(top, HD // 2, 1) + low
                else:
                    o = top + pltpu.roll(low, HD // 2, 1)
                o = o / totals[i, rows, :]
                obuf[half, xq, 4 * s + w] = paired(o[: PART // 2], o[PART // 2 :])[half]
            for w in range(4):
                o_copy(half, 4 * i + w, xq, 4 * s + w, False)
            return 0

        def v_step(t, work):
            def step(k, _):
                by_role(lambda role: pass_on(role, t, k, (0, 2)), both)
                lax.fori_loop(4 * k - 8, 4 * k - 6, work, 0)
                by_role(lambda role: pass_on(role, t, k, (1,)), both)
                if t == 1:

                    @pl.when(k == 2)
                    def _():
                        by_role(lambda role: own_part(role, 2), both)

                lax.fori_loop(4 * k - 6, 4 * k - 4, work, 0)
                by_role(lambda role: late_pair(role, t, k - 1), both)
                return 0

            return step

        for j in range(1, X):
            list_arrival(j).wait_recv()
        lrecv[pl.ds(x, 1)] = lsend[...][None]
        copy = pltpu.make_async_copy(lrecv, lists, l_copy.at[0])
        copy.start()
        copy.wait()
        pltpu.make_async_copy(qbuf, qbuf, q_recv.at[0]).wait()

        lax.fori_loop(2, 4, v_step(1, scores), 0)
        by_role(lambda role: turn(role, 1), both)
        lax.fori_loop(2, 4, v_step(2, lambda i, _: mix(0, i)), 0)

        def v_end(role):
            late_pair(role, 2, 3)
            pass_on(role, 2, 4)
            late(role, 2, 4)
            from_sibling(role, 2)

        by_role(v_end, both)
        lax.fori_loop(0, 8, lambda i, _: mix(1, i), 0)

        def done(role):
            for t in (0, 1, 2):
                ring_sent(role, t)

        by_role(done, both)

        def sent(i, _):
            xq, s = cluster(i)
            for half in (0, 1):
                for w in range(4):
                    o_copy(half, 4 * i + w, xq, 4 * s + w, True)
            return 0

        lax.fori_loop(0, 8, sent, 0)

    @pl.when(x == HX)
    def _():
        pass_on(HELP, 1, 2)
        own_part(HELP, 2)
        pass_on(HELP, 1, 3)
        turn(HELP, 1)
        for k in range(2, 5):
            pass_on(HELP, 2, k)
        for j in range(1, X):
            list_arrival(j).wait_recv()
        for t in (0, 1, 2):
            ring_sent(HELP, t)

    for t in (0, 1, 2):
        all_rows(t, True)
    each_y(lambda i: q_copy(i, True))
    for j in range(1, X):
        list_copy(j).wait_send()
    for half in (0, 1):
        pltpu.make_async_copy(oin.at[half], oin.at[half], o_recv.at[half]).wait()
    for h in range(HEADS):
        cols = slice(h * HD, (h + 1) * HD)
        out_ref[0 : PART // 2, cols], out_ref[PART // 2 :, cols] = paired(
            oin[0, h].astype(jnp.float32), oin[1, h].astype(jnp.float32)
        )


def local(queries, keys, values, key_lists, key_fill):
    bf = jnp.bfloat16
    anywhere = pl.BlockSpec(memory_space=pl.ANY)
    dma = pltpu.SemaphoreType.DMA
    return pl.pallas_call(
        kernel,
        out_shape=jax.ShapeDtypeStruct(queries.shape, bf),
        in_specs=[
            anywhere, anywhere, anywhere,
            anywhere, anywhere,
        ],
        out_specs=pl.BlockSpec(memory_space=pltpu.VMEM),
        scratch_shapes=[
            pltpu.VMEM((PER, SEL), jnp.int32),
            pltpu.SMEM((X * Z * C * PER,), jnp.int32),
            pltpu.VMEM((PART, HEADS * HD), bf),
            pltpu.VMEM((PART, HEADS * HD), bf),
            pltpu.VMEM((PART, HEADS * HD), bf),
            pltpu.VMEM((HEADS, GROUPS, 32, HD), bf),
            pltpu.VMEM((HEADS, GROUPS, 16, HD), bf),
            pltpu.VMEM((HEADS, GROUPS, 16, HD), bf),
            pltpu.VMEM((Z * C * CHUNK, 32, HD), bf),
            pltpu.VMEM((Z * C * CHUNK, 16, HD), bf),
            pltpu.VMEM((Z * C * CHUNK, 16, HD), bf),
            pltpu.VMEM((X, BLOCK, HD), bf),
            pltpu.VMEM((2, X, Y, PART // 2, HD), bf),
            pltpu.VMEM((2, HEADS, PART // 2, HD), bf),
            pltpu.VMEM((KEYS, HD), bf),
            pltpu.VMEM((2 * X, CROWS, KEYS), bf),
            pltpu.VMEM((2 * X, CROWS, 1), jnp.float32),
            pltpu.VMEM((24, 128), jnp.int32),
            pltpu.VMEM((X, 24, 128), jnp.int32),
            pltpu.SMEM((X, 24, 128), jnp.int32),
            dma((5,)),
            dma((4, HEADS)),
            dma((3, 3)),
            dma((1,)),
            dma((3,)),
            dma((3, 2, 3, 4)),
            dma((3,)),
            dma((3, Z, 2)),
            dma((3,)),
            dma((3, Z, 2)),
            dma((3,)),
            dma((3, Z)),
            dma((X - 1,)),
            dma((X - 1,)),
            dma((1,)),
            dma((2, X * Y)),
            dma((2,)),
        ],
        compiler_params=pltpu.CompilerParams(
            collective_id=0, has_side_effects=True, vmem_limit_bytes=56 * 1024 * 1024
        ),
        cost_estimate=pl.CostEstimate(flops=5_000_000_000, bytes_accessed=4_000_000, transcendentals=4_800_000),
    )(queries, keys, values, key_lists, key_fill)


def solution(mesh):
    in_specs = (
        P(("blk", "uly"), None),
        P(("blk", "uly"), None),
        P(("blk", "uly"), None),
        P("blk", None),
        P(),
    )
    out_specs = P(("blk", "uly"), None)
    return jax.shard_map(local, mesh=mesh, in_specs=in_specs, out_specs=out_specs, check_vma=False)
```
